128 devices in a mesh: rows: 32 (over y, x, z_lo), band: 4 (over z_hi, core).
Axes of the slice: x: 4, y: 4, z: 4 (z_hi: 2, z_lo: 2; z = z_hi * 2 + z_lo), core: 2. Of those that a mesh axis runs over, the one named last changes fastest.
Arguments:
- features: bfloat16 [8192, 128], P(('rows', 'band')), may hold values from -6 to 6
- deleted: int32 [8192], P(('rows', 'band')), may hold values 0 or 1
- proj_weight: bfloat16 [128, 64], replicated, may hold values from -0.5 to 0.5
- distance_embed: float32 [32, 128], P(None, 'band'), may hold values from -3 to 3
- conv_weight: float32 [8, 9, 32, 32], replicated, may hold values from -0.375 to 0.375
- conv_bias: float32 [8, 32], replicated, may hold values from -1.5 to 1.5
- dilations: int32 [4], replicated, may hold values from 1 to 8, as said below
Outputs:
- trunk_map: float32 [32, 128, 8192], P(None, 'band', 'rows')
The draws below stay inside these ranges and needn't reach their ends.
Inputs may be any that keep to these rules, and one draw needn't show every extreme that they name: `dilations`: 8 occurs in every draw.
All inputs are finite; a program needn't handle non-finite values. No bound on the sum of `deleted` on one device may be relied on, other than what follows from the above.
Results may differ from the reference program's by a relative error of at most 0.00065.
Values may be sent and summed in bfloat16 or wider, within the bound.
A program may use at most 64 MiB of HBM per device.

```python
import jax
import jax.numpy as jnp
from jax import lax

CH = 128
PC = 32
MAXDIL = 8
BLOCKS = 4
BINS = 8192
DIAGS = 128


def draw_dilations(key, part):
    key = jax.random.fold_in(key, 7)
    key_values = jax.random.fold_in(key, 1)
    key_where = jax.random.fold_in(key, 2)
    plan = jax.random.randint(key_values, (BLOCKS,), 1, MAXDIL + 1, dtype=jnp.int32)
    position = jax.random.randint(key_where, (), 0, BLOCKS, dtype=jnp.int32)
    places = jnp.arange(BLOCKS, dtype=jnp.int32)
    return jnp.where(places == position, jnp.int32(MAXDIL), plan).astype(jnp.int32)


def plant(result, stream_key, least, top_value):
    longest = result.shape.index(max(result.shape))
    spots = []
    for shift in (0, 1):
        where = [jax.random.randint(jax.random.fold_in(stream_key, axis), (), 0, length) for axis, length in enumerate(result.shape)]
        where[longest] = (where[longest] + shift) % result.shape[longest]
        spots.append(tuple(where))
    return result.at[spots[0]].set(least).at[spots[1]].set(top_value)


def steps_of(key, shape, pieces, smallest, high):
    loudness = 1.0
    for dim, shards_of in pieces:
        steps = jax.random.uniform(jax.random.fold_in(jax.random.fold_in(key, 6), dim), (shards_of,), jnp.float32, smallest / len(pieces), high / len(pieces))
        loudness = loudness * jnp.repeat(jnp.exp(steps), shape[dim] // shards_of).reshape((-1,) + (1,) * (len(shape) - 1 - dim))
    return loudness


def noise(stream_key, dims, spread, reach, pieces=(), held_as=jnp.bfloat16):
    factor_of = steps_of(stream_key, dims, pieces, -0.22, 0.18) if pieces else 1.0
    result = jax.random.normal(stream_key, dims, jnp.float32) * spread * factor_of
    return jnp.minimum(jnp.maximum(result, -reach), reach).astype(held_as)


def setup_inputs(seed: int = 0) -> dict:
    seeds = jax.random.split(jax.random.key(seed), 8)
    features = noise(seeds[0], (BINS, CH), 1.0, 6.0, ((0, 128),))
    deleted = plant((jax.random.randint(seeds[1], (BINS,), 0, 8) < 1).astype(jnp.int32), jax.random.fold_in(seeds[1], 1), 0, 1)
    proj_weight = noise(seeds[2], (CH, 2 * PC), CH ** -0.5, 0.5)
    distance_embed = noise(seeds[3], (PC, DIAGS), 0.5, 3.0, ((1, 4),), jnp.float32)
    conv_weight = noise(seeds[4], (2 * BLOCKS, 9, PC, PC), (9 * PC) ** -0.5, 0.375, (), jnp.float32)
    conv_bias = noise(seeds[5], (2 * BLOCKS, PC), 0.3, 1.5, (), jnp.float32)
    dilations = draw_dilations(jax.random.fold_in(seeds[7], 71), 0)
    return dict(features=features, deleted=deleted, proj_weight=proj_weight, distance_embed=distance_embed, conv_weight=conv_weight, conv_bias=conv_bias, dilations=dilations)


precise = lax.Precision.HIGHEST


def conv_layer(trunk_map, weights, biases, dilation):
    padded = jnp.pad(trunk_map, ((0, 0), (MAXDIL, MAXDIL), (MAXDIL, MAXDIL)))
    anchor = jnp.zeros((), jnp.int32)
    summed = jnp.zeros(trunk_map.shape, jnp.float32)
    for diag_step in (-1, 0, 1):
        for bin_step in (-1, 0, 1):
            tap_index = 3 * (diag_step + 1) + (bin_step + 1)
            start_diag = (MAXDIL + dilation * diag_step).astype(jnp.int32)
            start_bin = (MAXDIL + dilation * bin_step).astype(jnp.int32)
            window = lax.dynamic_slice(padded, (anchor, start_diag, start_bin), trunk_map.shape)
            summed = summed + jnp.einsum("oc,cdi->odi", weights[tap_index], window, precision=precise)
    return summed + biases[:, None, None]


def residual_block(trunk_map, conv_weight, conv_bias, dilation, valid_mask, layer):
    branch = conv_layer(jax.nn.relu(trunk_map), conv_weight[2 * layer], conv_bias[2 * layer], dilation) * valid_mask
    branch = conv_layer(jax.nn.relu(branch), conv_weight[2 * layer + 1], conv_bias[2 * layer + 1], dilation) * valid_mask
    return trunk_map + branch


def symmetrize(trunk_map, valid_mask, column_index):
    half_band = DIAGS // 2
    extended = jnp.concatenate([trunk_map, jnp.zeros((PC, 1, BINS), jnp.float32)], axis=1)
    mirrored = extended[:, ::-1, :][:, :DIAGS, :]
    padded = jnp.pad(mirrored, ((0, 0), (0, 0), (half_band, half_band)))
    diag_rows = jnp.arange(DIAGS, dtype=jnp.int32)[:, None]
    partner_map = padded[:, diag_rows, column_index]
    return 0.5 * (trunk_map + partner_map) * valid_mask


def reference(features, deleted, proj_weight, distance_embed, conv_weight, conv_bias, dilations):
    half_band = DIAGS // 2
    kept_bins = (1 - deleted).astype(jnp.bfloat16)
    masked = features * kept_bins[:, None]
    projected = jnp.dot(masked, proj_weight, preferred_element_type=jnp.float32)
    row_part = projected[:, :PC].T
    col_part = projected[:, PC:].T
    diag_iota = jnp.arange(DIAGS, dtype=jnp.int32)[:, None]
    bin_iota = jnp.arange(BINS, dtype=jnp.int32)[None, :]
    column_index = bin_iota + diag_iota
    target = column_index - half_band
    valid_mask = ((target >= 0) & (target < BINS)).astype(jnp.float32)
    col_padded = jnp.pad(col_part, ((0, 0), (half_band, half_band)))
    col_values = col_padded[:, column_index]
    trunk_map = jax.nn.relu(row_part[:, None, :] + col_values + distance_embed[:, :, None]) * valid_mask
    for layer in range(BLOCKS):
        if layer == BLOCKS // 2:
            trunk_map = symmetrize(trunk_map, valid_mask, column_index)
        trunk_map = residual_block(trunk_map, conv_weight, conv_bias, dilations[layer], valid_mask, layer)
    return trunk_map
```

```python
import functools

import jax
import jax.numpy as jnp
from jax import lax
from jax.experimental import pallas as pl
from jax.experimental.pallas import tpu as pltpu
from jax.sharding import PartitionSpec as P

PC = 32
DIAGS = 128
HALF = 64
BAND = 32
BINW = 256
MAXDIL = 8
BINS = 8192
W1 = 512
W2 = 384
FW = 640
R = 96
PAD = 8


def split_store(y_ref, j, x):
    hi = x.astype(jnp.bfloat16)
    lo = (x - hi.astype(jnp.float32)).astype(jnp.bfloat16)
    y_ref[j, 0:PC, :] = hi
    y_ref[j, PC:2 * PC, :] = lo


def taps(y_ref, j, k, weights):
    rows = jnp.concatenate([y_ref[j - k], y_ref[j], y_ref[j + k]], axis=0)
    return jnp.dot(weights, rows, preferred_element_type=jnp.float32)


def gather_taps(p, k, bias):
    width = p.shape[1]
    parts = [p[64 * b:64 * b + 32] + p[64 * b + 32:64 * b + 64] for b in range(3)]
    return (
        parts[1]
        + pltpu.roll(parts[0], k, 1)
        + pltpu.roll(parts[2], width - k, 1)
        + bias
    )


def valid_of(u, bins):
    low = jnp.maximum(0, HALF - u)
    high = jnp.where((u >= 0) & (u < DIAGS), jnp.minimum(BINS, BINS + HALF - u), 0)
    return (bins >= low) & (bins < high)


def blocks(dil_ref, first_block, w_ref, bias_ref, v_ref, ya, yb, first_u, bin0, width, rows_of, unroll):
    bins = lax.broadcasted_iota(jnp.int32, (1, width), 1) + bin0
    for n in range(4):
        k = dil_ref[first_block + n // 2]
        weights = w_ref[n]
        bias = jnp.broadcast_to(bias_ref[n], (PC, width))
        src, dst = (ya, yb) if n % 2 == 0 else (yb, ya)
        start, count = rows_of(n)

        def step(t, carry, n=n, k=k, weights=weights, bias=bias, src=src, dst=dst, start=start):
            base = start + t * unroll
            for s in range(unroll):
                j = base + s
                valid = valid_of(first_u + j, bins)
                branch = gather_taps(taps(src, j + PAD, k, weights), k, bias)
                branch = jnp.where(valid, branch, 0.0)
                if n % 2 == 1:
                    branch = v_ref[j] + branch
                    v_ref[j] = branch
                if n < 3:
                    split_store(dst, j + PAD, jnp.maximum(branch, 0.0))
            return carry

        lax.fori_loop(0, count // unroll, step, 0)


def first_half(dil_ref, meta_ref, feat_ref, proj_ref, emb_ref, w_ref, bias_ref, out_ref, v_ref, ya, yb, row_s, col_s, sem):
    half = meta_ref[0]
    bin0 = meta_ref[1] - 128
    first_u = half * 32
    projected = lax.dot_general(
        proj_ref[...], feat_ref[...], (((1,), (1,)), ((), ())), preferred_element_type=jnp.float32
    )
    row_s[...] = projected[:PC, 64:64 + W1]
    col_s[...] = projected[PC:]
    zero = jnp.zeros((PAD, 2 * PC, W1), jnp.bfloat16)
    for y in (ya, yb):
        y[0:PAD] = zero
        y[PAD + R:] = zero
    bins = lax.broadcasted_iota(jnp.int32, (1, W1), 1) + bin0
    lanes = lax.broadcasted_iota(jnp.int32, (PC, DIAGS), 1)

    def init(j, carry):
        u = first_u + j
        col = pltpu.roll(col_s[...], FW - u, 1)[:, :W1]
        emb = jnp.sum(jnp.where(lanes == u, emb_ref[...], 0.0), axis=1, keepdims=True)
        x = jnp.maximum(row_s[...] + col + emb, 0.0)
        x = jnp.where(valid_of(u, bins), x, 0.0)
        v_ref[j] = x
        split_store(ya, j + PAD, x)
        return carry

    lax.fori_loop(0, R, init, 0)

    def rows_of(n):
        return half * (8 * n + 8), 88 - 8 * n

    blocks(dil_ref, 0, w_ref, bias_ref, v_ref, ya, yb, first_u, bin0, W1, rows_of, 2)
    copy = pltpu.make_async_copy(v_ref.at[pl.ds(half * 32, 64)], out_ref, sem)
    copy.start()
    copy.wait()


def second_half(dil_ref, meta_ref, own_ref, other_ref, w_ref, bias_ref, out_ref, m_ref, v_ref, ya, yb, o_ref, sem, osem):
    half = meta_ref[0]
    bin0 = meta_ref[1] - 64
    first_u = meta_ref[2] * BAND - 32
    c1 = pltpu.make_async_copy(own_ref, m_ref.at[pl.ds(half * 64, 64)], sem.at[0])
    c2 = pltpu.make_async_copy(other_ref, m_ref.at[pl.ds(64 - half * 64, 64)], sem.at[1])
    c1.start()
    c2.start()
    zero = jnp.zeros((PAD, 2 * PC, W2), jnp.bfloat16)
    for y in (ya, yb):
        y[0:PAD] = zero
        y[PAD + R:] = zero
    c1.wait()
    c2.wait()
    bins = lax.broadcasted_iota(jnp.int32, (1, W2), 1) + bin0

    def init(j, carry):
        u = first_u + j
        ui = jnp.clip(u, 0, DIAGS - 1)
        own = pltpu.roll(m_ref[ui], W1 - 64, 1)[:, :W2]
        pi = jnp.clip(DIAGS - u, 0, DIAGS - 1)
        partner = pltpu.roll(m_ref[pi], (W1 - ui) % W1, 1)[:, :W2]
        partner = jnp.where(u > 0, partner, 0.0)
        x = jnp.where(valid_of(u, bins), 0.5 * (own + partner), 0.0)
        v_ref[j] = x
        split_store(ya, j + PAD, jnp.maximum(x, 0.0))
        return carry

    lax.fori_loop(0, R, init, 0)

    def rows_of(n):
        return 8 * n + 8, 80 - 16 * n

    blocks(dil_ref, 2, w_ref, bias_ref, v_ref, ya, yb, first_u, bin0, W2, rows_of, 2)
    for j in range(BAND):
        o_ref[j] = pltpu.roll(v_ref[32 + j], W2 - 64, 1)[:, :BINW]
        pltpu.make_async_copy(o_ref.at[j], out_ref.at[:, j, :], osem.at[j]).start()
    for j in range(BAND):
        pltpu.make_async_copy(o_ref.at[j], out_ref.at[:, j, :], osem.at[j]).wait()


smem = pl.BlockSpec(memory_space=pltpu.SMEM)
vmem = pl.BlockSpec(memory_space=pltpu.VMEM)
hbm = pl.BlockSpec(memory_space=pl.ANY)
LIMIT = 56 * 2 ** 20


def run_first(dil, meta, feat, proj, emb, w, bias):
    return pl.pallas_call(
        first_half,
        out_shape=jax.ShapeDtypeStruct((64, PC, W1), jnp.float32),
        in_specs=[smem, smem, vmem, vmem, vmem, vmem, vmem],
        out_specs=hbm,
        scratch_shapes=[
            pltpu.VMEM((R, PC, W1), jnp.float32),
            pltpu.VMEM((R + 2 * PAD, 2 * PC, W1), jnp.bfloat16),
            pltpu.VMEM((R + 2 * PAD, 2 * PC, W1), jnp.bfloat16),
            pltpu.VMEM((PC, W1), jnp.float32),
            pltpu.VMEM((PC, FW), jnp.float32),
            pltpu.SemaphoreType.DMA,
        ],
        compiler_params=pltpu.CompilerParams(vmem_limit_bytes=LIMIT),
        name="first_half",
    )(dil, meta, feat, proj, emb, w, bias)


def run_second(dil, meta, own, other, w, bias):
    return pl.pallas_call(
        second_half,
        out_shape=jax.ShapeDtypeStruct((PC, BAND, BINW), jnp.float32),
        in_specs=[smem, smem, hbm, hbm, vmem, vmem],
        out_specs=hbm,
        scratch_shapes=[
            pltpu.VMEM((DIAGS, PC, W1), jnp.float32),
            pltpu.VMEM((R, PC, W2), jnp.float32),
            pltpu.VMEM((R + 2 * PAD, 2 * PC, W2), jnp.bfloat16),
            pltpu.VMEM((R + 2 * PAD, 2 * PC, W2), jnp.bfloat16),
            pltpu.VMEM((BAND, PC, BINW), jnp.float32),
            pltpu.SemaphoreType.DMA((2,)),
            pltpu.SemaphoreType.DMA((BAND,)),
        ],
        compiler_params=pltpu.CompilerParams(vmem_limit_bytes=LIMIT),
        name="second_half",
    )(dil, meta, own, other, w, bias)


def prepare_weights(conv_weight):
    w = conv_weight.reshape(8, 3, 3, PC, PC).transpose(0, 2, 3, 1, 4)
    high = lax.reduce_precision(w, 8, 7)
    low = w - high
    both = jnp.stack([high, low], axis=2).astype(jnp.bfloat16)
    both = jnp.broadcast_to(both[:, :, :, :, :, None, :], (8, 3, 2, PC, 3, 2, PC))
    return both.reshape(8, 192, 192)


def body(features, deleted, proj_weight, distance_embed, conv_weight, conv_bias, dilations):
    band = lax.axis_index("band")
    row = lax.axis_index("rows")
    count = lax.axis_size("rows")
    kept = (1 - deleted).astype(jnp.bfloat16)
    masked = features * kept[:, None]
    own = lax.all_gather(masked, "band", axis=0, tiled=True)
    up = [(i, i + 1) for i in range(count - 1)]
    down = [(i + 1, i) for i in range(count - 1)]
    before = lax.ppermute(own[BINW - 192:], "rows", up)
    after = lax.ppermute(own[:192], "rows", down)
    feat = jnp.concatenate([before, own, after], axis=0)
    emb = lax.all_gather(distance_embed, "band", axis=1, tiled=True)
    w = prepare_weights(conv_weight)
    bias = conv_bias[:, :, None]
    meta = jnp.stack([band % 2, row * BINW, band]).astype(jnp.int32)
    mine = run_first(dilations, meta, feat, proj_weight.T, emb, w[:4], bias[:4])
    other = lax.ppermute(mine, "band", [(0, 1), (1, 0), (2, 3), (3, 2)])
    return run_second(dilations, meta, mine, other, w[4:], bias[4:])


def solution(mesh):
    return jax.shard_map(
        body,
        mesh=mesh,
        in_specs=(
            P(("rows", "band"), None),
            P(("rows", "band")),
            P(),
            P(None, "band"),
            P(),
            P(),
            P(),
        ),
        out_specs=P(None, "band", "rows"),
        check_vma=False,
    )
```

```python
import functools

import jax
import jax.numpy as jnp
from jax import lax
from jax.experimental import pallas as pl
from jax.experimental.pallas import tpu as pltpu
from jax.sharding import PartitionSpec as P

PC = 32
DIAGS = 128
HALF = 64
BAND = 32
BINW = 256
MAXDIL = 8
BINS = 8192
W1 = 512
W2 = 384
FW = 640
R = 96
PAD = 8


def split_store(y_ref, j, x):
    hi = x.astype(jnp.bfloat16)
    lo = (x - hi.astype(jnp.float32)).astype(jnp.bfloat16)
    y_ref[j, 0:PC, :] = hi
    y_ref[j, PC:2 * PC, :] = lo


def taps(y_ref, j, k, weights):
    rows = jnp.concatenate([y_ref[j - k], y_ref[j], y_ref[j + k]], axis=0)
    return jnp.dot(weights, rows, preferred_element_type=jnp.float32)


def gather_taps(p, k, bias):
    width = p.shape[1]
    parts = [p[64 * b:64 * b + 32] + p[64 * b + 32:64 * b + 64] for b in range(3)]
    return (
        parts[1]
        + pltpu.roll(parts[0], k, 1)
        + pltpu.roll(parts[2], width - k, 1)
        + bias
    )


def valid_of(u, bins):
    low = jnp.maximum(0, HALF - u)
    high = jnp.where((u >= 0) & (u < DIAGS), jnp.minimum(BINS, BINS + HALF - u), 0)
    return (bins >= low) & (bins < high)


def blocks(dil_ref, first_block, w_ref, bias_ref, v_ref, ya, yb, first_u, bin0, width, rows_of, unroll):
    bins = lax.broadcasted_iota(jnp.int32, (1, width), 1) + bin0
    for n in range(4):
        k = dil_ref[first_block + n // 2]
        weights = w_ref[n]
        bias = jnp.broadcast_to(bias_ref[n], (PC, width))
        src, dst = (ya, yb) if n % 2 == 0 else (yb, ya)
        start, count = rows_of(n)

        def step(t, carry, n=n, k=k, weights=weights, bias=bias, src=src, dst=dst, start=start):
            base = start + t * unroll
            for s in range(unroll):
                j = base + s
                valid = valid_of(first_u + j, bins)
                branch = gather_taps(taps(src, j + PAD, k, weights), k, bias)
                branch = jnp.where(valid, branch, 0.0)
                if n % 2 == 1:
                    branch = v_ref[j] + branch
                    v_ref[j] = branch
                if n < 3:
                    split_store(dst, j + PAD, jnp.maximum(branch, 0.0))
            return carry

        lax.fori_loop(0, count // unroll, step, 0)


def first_half(dil_ref, meta_ref, feat_ref, proj_ref, emb_ref, w_ref, bias_ref, out_ref, v_ref, ya, yb, row_s, col_s, sem):
    half = meta_ref[0]
    bin0 = meta_ref[1] - 128
    first_u = half * 32
    projected = lax.dot_general(
        proj_ref[...], feat_ref[...], (((1,), (1,)), ((), ())), preferred_element_type=jnp.float32
    )
    row_s[...] = projected[:PC, 64:64 + W1]
    col_s[...] = projected[PC:]
    zero = jnp.zeros((PAD, 2 * PC, W1), jnp.bfloat16)
    for y in (ya, yb):
        y[0:PAD] = zero
        y[PAD + R:] = zero
    bins = lax.broadcasted_iota(jnp.int32, (1, W1), 1) + bin0
    lanes = lax.broadcasted_iota(jnp.int32, (PC, DIAGS), 1)

    def init(t, carry):
        for s in range(4):
            start(t * 4 + s)
        return carry

    def start(j):
        u = first_u + j
        col = pltpu.roll(col_s[...], FW - u, 1)[:, :W1]
        emb = jnp.sum(jnp.where(lanes == u, emb_ref[...], 0.0), axis=1, keepdims=True)
        x = jnp.maximum(row_s[...] + col + emb, 0.0)
        x = jnp.where(valid_of(u, bins), x, 0.0)
        v_ref[j] = x
        split_store(ya, j + PAD, x)

    lax.fori_loop(0, R // 4, init, 0)

    def rows_of(n):
        return half * (8 * n + 8), 88 - 8 * n

    blocks(dil_ref, 0, w_ref, bias_ref, v_ref, ya, yb, first_u, bin0, W1, rows_of, 8)
    copy = pltpu.make_async_copy(v_ref.at[pl.ds(half * 32, 64)], out_ref, sem)
    copy.start()
    copy.wait()


def second_half(dil_ref, meta_ref, own_ref, other_ref, w_ref, bias_ref, out_ref, m_ref, v_ref, ya, yb, o_ref, sem, osem):
    half = meta_ref[0]
    bin0 = meta_ref[1] - 64
    first_u = meta_ref[2] * BAND - 32
    c1 = pltpu.make_async_copy(own_ref, m_ref.at[pl.ds(half * 64, 64)], sem.at[0])
    c2 = pltpu.make_async_copy(other_ref, m_ref.at[pl.ds(64 - half * 64, 64)], sem.at[1])
    c1.start()
    c2.start()
    zero = jnp.zeros((PAD, 2 * PC, W2), jnp.bfloat16)
    for y in (ya, yb):
        y[0:PAD] = zero
        y[PAD + R:] = zero
    c1.wait()
    c2.wait()
    bins = lax.broadcasted_iota(jnp.int32, (1, W2), 1) + bin0

    def init(t, carry):
        for s in range(4):
            start(t * 4 + s)
        return carry

    def start(j):
        u = first_u + j
        ui = jnp.clip(u, 0, DIAGS - 1)
        own = pltpu.roll(m_ref[ui], W1 - 64, 1)[:, :W2]
        pi = jnp.clip(DIAGS - u, 0, DIAGS - 1)
        partner = pltpu.roll(m_ref[pi], (W1 - ui) % W1, 1)[:, :W2]
        partner = jnp.where(u > 0, partner, 0.0)
        x = jnp.where(valid_of(u, bins), 0.5 * (own + partner), 0.0)
        v_ref[j] = x
        split_store(ya, j + PAD, jnp.maximum(x, 0.0))

    lax.fori_loop(0, R // 4, init, 0)

    def rows_of(n):
        return 8 * n + 8, 80 - 16 * n

    blocks(dil_ref, 2, w_ref, bias_ref, v_ref, ya, yb, first_u, bin0, W2, rows_of, 8)
    for j in range(BAND):
        o_ref[j] = pltpu.roll(v_ref[32 + j], W2 - 64, 1)[:, :BINW]
        pltpu.make_async_copy(o_ref.at[j], out_ref.at[:, j, :], osem.at[j]).start()
    for j in range(BAND):
        pltpu.make_async_copy(o_ref.at[j], out_ref.at[:, j, :], osem.at[j]).wait()


smem = pl.BlockSpec(memory_space=pltpu.SMEM)
vmem = pl.BlockSpec(memory_space=pltpu.VMEM)
hbm = pl.BlockSpec(memory_space=pl.ANY)
LIMIT = 56 * 2 ** 20


def run_first(dil, meta, feat, proj, emb, w, bias):
    return pl.pallas_call(
        first_half,
        out_shape=jax.ShapeDtypeStruct((64, PC, W1), jnp.float32),
        in_specs=[smem, smem, vmem, vmem, vmem, vmem, vmem],
        out_specs=hbm,
        scratch_shapes=[
            pltpu.VMEM((R, PC, W1), jnp.float32),
            pltpu.VMEM((R + 2 * PAD, 2 * PC, W1), jnp.bfloat16),
            pltpu.VMEM((R + 2 * PAD, 2 * PC, W1), jnp.bfloat16),
            pltpu.VMEM((PC, W1), jnp.float32),
            pltpu.VMEM((PC, FW), jnp.float32),
            pltpu.SemaphoreType.DMA,
        ],
        compiler_params=pltpu.CompilerParams(vmem_limit_bytes=LIMIT),
        name="first_half",
    )(dil, meta, feat, proj, emb, w, bias)


def run_second(dil, meta, own, other, w, bias):
    return pl.pallas_call(
        second_half,
        out_shape=jax.ShapeDtypeStruct((PC, BAND, BINW), jnp.float32),
        in_specs=[smem, smem, hbm, hbm, vmem, vmem],
        out_specs=hbm,
        scratch_shapes=[
            pltpu.VMEM((DIAGS, PC, W1), jnp.float32),
            pltpu.VMEM((R, PC, W2), jnp.float32),
            pltpu.VMEM((R + 2 * PAD, 2 * PC, W2), jnp.bfloat16),
            pltpu.VMEM((R + 2 * PAD, 2 * PC, W2), jnp.bfloat16),
            pltpu.VMEM((BAND, PC, BINW), jnp.float32),
            pltpu.SemaphoreType.DMA((2,)),
            pltpu.SemaphoreType.DMA((BAND,)),
        ],
        compiler_params=pltpu.CompilerParams(vmem_limit_bytes=LIMIT),
        name="second_half",
    )(dil, meta, own, other, w, bias)


def prepare_weights(conv_weight):
    w = conv_weight.reshape(8, 3, 3, PC, PC).transpose(0, 2, 3, 1, 4)
    high = lax.reduce_precision(w, 8, 7)
    low = w - high
    both = jnp.stack([high, low], axis=2).astype(jnp.bfloat16)
    both = jnp.broadcast_to(both[:, :, :, :, :, None, :], (8, 3, 2, PC, 3, 2, PC))
    return both.reshape(8, 192, 192)


def body(features, deleted, proj_weight, distance_embed, conv_weight, conv_bias, dilations):
    band = lax.axis_index("band")
    row = lax.axis_index("rows")
    count = lax.axis_size("rows")
    kept = (1 - deleted).astype(jnp.bfloat16)
    masked = features * kept[:, None]
    own = lax.all_gather(masked, "band", axis=0, tiled=True)
    up = [(i, i + 1) for i in range(count - 1)]
    down = [(i + 1, i) for i in range(count - 1)]
    before = lax.ppermute(own[BINW - 192:], "rows", up)
    after = lax.ppermute(own[:192], "rows", down)
    feat = jnp.concatenate([before, own, after], axis=0)
    emb = lax.all_gather(distance_embed, "band", axis=1, tiled=True)
    w = prepare_weights(conv_weight)
    bias = conv_bias[:, :, None]
    meta = jnp.stack([band % 2, row * BINW, band]).astype(jnp.int32)
    mine = run_first(dilations, meta, feat, proj_weight.T, emb, w[:4], bias[:4])
    other = lax.ppermute(mine, "band", [(0, 1), (1, 0), (2, 3), (3, 2)])
    return run_second(dilations, meta, mine, other, w[4:], bias[4:])


def solution(mesh):
    return jax.shard_map(
        body,
        mesh=mesh,
        in_specs=(
            P(("rows", "band"), None),
            P(("rows", "band")),
            P(),
            P(None, "band"),
            P(),
            P(),
            P(),
        ),
        out_specs=P(None, "band", "rows"),
        check_vma=False,
    )
```

```python
import functools

import jax
import jax.numpy as jnp
from jax import lax
from jax.experimental import pallas as pl
from jax.experimental.pallas import tpu as pltpu
from jax.sharding import PartitionSpec as P

PC = 32
DIAGS = 128
HALF = 64
BAND = 32
BINW = 256
MAXDIL = 8
BINS = 8192
W1 = 512
W2 = 384
FW = 640
R = 96
PAD = 8
UNROLL = 16
ROWS = 32
MESH = pl.DeviceIdType.MESH


def split_store(y_ref, j, x):
    hi = x.astype(jnp.bfloat16)
    lo = (x - hi.astype(jnp.float32)).astype(jnp.bfloat16)
    y_ref[j, 0:PC, :] = hi
    y_ref[j, PC:2 * PC, :] = lo


def gather_taps(p, k, bias):
    width = p.shape[1]
    parts = [p[64 * b:64 * b + 32] + p[64 * b + 32:64 * b + 64] for b in range(3)]
    return (
        parts[1]
        + pltpu.roll(parts[0], k, 1)
        + pltpu.roll(parts[2], width - k, 1)
        + bias
    )


def valid_of(u, bins):
    low = jnp.maximum(0, HALF - u)
    high = jnp.where((u >= 0) & (u < DIAGS), jnp.minimum(BINS, BINS + HALF - u), 0)
    return (bins >= low) & (bins < high)


def conv(k, weights, bias, src, dst, v_ref, first_u, bins, start, count, residual, done=None):
    width = bins.shape[1]
    cat = 2 if width % 256 else 1

    def group(base, rows):
        for g in range(0, rows, cat):
            stack = [
                jnp.concatenate([src[j - k], src[j], src[j + k]], axis=0)
                for j in [base + g + c + PAD for c in range(cat)]
            ]
            stack = stack[0] if cat == 1 else jnp.concatenate(stack, axis=1)
            p = jnp.dot(weights, stack, preferred_element_type=jnp.float32)
            for c in range(cat):
                j = base + g + c
                branch = gather_taps(p[:, c * width:(c + 1) * width], k, bias)
                branch = jnp.where(valid_of(first_u + j, bins), branch, 0.0)
                if residual:
                    branch = v_ref[j] + branch
                    v_ref[j] = branch
                if dst is not None:
                    split_store(dst, j + PAD, jnp.maximum(branch, 0.0))
        if done is not None:
            done(base, rows)

    def step(t, carry):
        group(start + t * UNROLL, UNROLL)
        return carry

    lax.fori_loop(0, count // UNROLL, step, 0)
    if count % UNROLL:
        group(start + count // UNROLL * UNROLL, count % UNROLL)


def blocks(dil_ref, first_block, w_ref, bias_ref, v_ref, ya, yb, first_u, bins, rows_of, done=None):
    for n in range(4):
        src, dst = (ya, yb) if n % 2 == 0 else (yb, ya)
        start, count = rows_of(n)
        bias = jnp.concatenate([bias_ref[n]] * (bins.shape[1] // 128), axis=1)
        conv(
            dil_ref[first_block + n // 2], w_ref[n], bias, src, dst if n < 3 else None, v_ref,
            first_u, bins, start, count, n % 2 == 1, done if n == 3 else None,
        )


def gather(feat_ref, del_ref, emb_ref, cw_ref, cb_ref, feat_out, emb_out, w_first, w_second, bias_first, bias_second,
           kept, land, emb_land, send, recv, esend, erecv):
    row = lax.axis_index("rows")
    band = lax.axis_index("band")
    near = [(row, lax.rem(band + d, 4)) for d in range(1, 4)]
    after = [(lax.rem(row + 1, ROWS), d) for d in range(4)]
    before = [(lax.rem(row + ROWS - 1, ROWS), d) for d in range(4)]
    barrier = pltpu.get_barrier_semaphore()
    for r, b in near + after + before:
        pl.semaphore_signal(barrier, inc=1, device_id={"rows": r, "band": b}, device_id_type=MESH)

    same = lax.broadcasted_iota(jnp.int32, (64, 64), 0) == lax.broadcasted_iota(jnp.int32, (64, 64), 1)
    gone = jnp.sum(jnp.where(same, del_ref[...].astype(jnp.float32), 0.0), axis=1, keepdims=True)
    kept[...] = (feat_ref[...].astype(jnp.float32) * (1.0 - gone)).astype(jnp.bfloat16)

    pl.semaphore_wait(barrier, 11)
    copies = []

    def send_to(r, b, slot, index):
        copies.append(pltpu.make_async_remote_copy(
            kept, land.at[slot, band], send.at[index], recv.at[slot, band],
            device_id={"rows": r, "band": b}, device_id_type=MESH))

    for d, (r, b) in enumerate(near):
        send_to(r, b, 1, d)
    for d, (r, b) in enumerate(after):
        send_to(r, b, 0, 3 + d)
    for d, (r, b) in enumerate(before):
        send_to(r, b, 2, 7 + d)
    for d, (r, b) in enumerate(near):
        copies.append(pltpu.make_async_remote_copy(
            emb_ref, emb_land.at[band], esend.at[d], erecv.at[band],
            device_id={"rows": r, "band": b}, device_id_type=MESH))
    for copy in copies:
        copy.start()
    land[1, band] = kept[...]
    emb_land[band] = emb_ref[...]

    square = lax.broadcasted_iota(jnp.int32, (PC, PC), 0) == lax.broadcasted_iota(jnp.int32, (PC, PC), 1)

    def weights(first, w_out, bias_out, n, carry):
        for b in range(3):
            t = [cw_ref[first + n, 3 * a + b] for a in range(3)]
            wide = jnp.concatenate([t[0], t[0], t[1], t[1], t[2], t[2]], axis=1)
            high = wide.astype(jnp.bfloat16)
            w_out[n, 64 * b:64 * b + 32, :] = high
            w_out[n, 64 * b + 32:64 * b + 64, :] = (wide - high.astype(jnp.float32)).astype(jnp.bfloat16)
        column = jnp.sum(jnp.where(square, cb_ref[first + n], 0.0), axis=1, keepdims=True)
        bias_out[n] = jnp.broadcast_to(column, (PC, 128))
        return carry

    lax.fori_loop(0, 4, functools.partial(weights, 0, w_first, bias_first), 0)
    lax.fori_loop(0, 4, functools.partial(weights, 4, w_second, bias_second), 0)

    def arrived(buf, sem):
        pltpu.make_async_copy(buf, buf, sem).wait()

    for d in range(1, 4):
        b = lax.rem(band + d, 4)
        arrived(land.at[1, b], recv.at[1, b])
        arrived(emb_land.at[b], erecv.at[b])
    for d in range(4):
        arrived(land.at[0, d], recv.at[0, d])
        arrived(land.at[2, d], recv.at[2, d])
    for i, (s, b) in enumerate([(0, 1), (0, 2), (0, 3), (1, 0), (1, 1), (1, 2), (1, 3), (2, 0), (2, 1), (2, 2)]):
        feat_out[64 * i:64 * i + 64] = land[s, b]
    emb_out[...] = emb_land[...]
    for copy in copies:
        copy.wait_send()


def first_half(dil_ref, feat_ref, proj_ref, emb_ref, w_ref, bias_ref, out_ref, v_ref, ya, yb, row_s, col_s, sem):
    half = lax.rem(lax.axis_index("band"), 2)
    bin0 = lax.axis_index("rows") * BINW - 128
    first_u = half * 32
    projected = lax.dot_general(
        proj_ref[...], feat_ref[...], (((0,), (1,)), ((), ())), preferred_element_type=jnp.float32
    )
    row_s[...] = projected[:PC, 64:64 + W1]
    col_s[...] = projected[PC:]
    zero = jnp.zeros((PAD, 2 * PC, W1), jnp.bfloat16)
    for y in (ya, yb):
        y[0:PAD] = zero
        y[PAD + R:] = zero
    bins = lax.broadcasted_iota(jnp.int32, (1, W1), 1) + bin0
    lanes = lax.broadcasted_iota(jnp.int32, (PC, BAND), 1)

    def init(t, carry):
        for s in range(4):
            start(t * 4 + s)
        return carry

    def start(j):
        u = first_u + j
        col = pltpu.roll(col_s[...], FW - u, 1)[:, :W1]
        emb = jnp.sum(jnp.where(lanes == lax.rem(u, BAND), emb_ref[lax.div(u, BAND)], 0.0), axis=1, keepdims=True)
        x = jnp.maximum(row_s[...] + col + emb, 0.0)
        x = jnp.where(valid_of(u, bins), x, 0.0)
        v_ref[j] = x
        split_store(ya, j + PAD, x)

    lax.fori_loop(0, R // 4, init, 0)

    def rows_of(n):
        return half * (8 * n + 8), 88 - 8 * n

    def out_copy(base, rows):
        return pltpu.make_async_copy(
            v_ref.at[pl.ds(base, rows)], out_ref.at[pl.ds(base - half * 32, rows)], sem)

    blocks(dil_ref, 0, w_ref, bias_ref, v_ref, ya, yb, first_u, bins, rows_of,
           lambda base, rows: out_copy(base, rows).start())
    out_copy(half * 32, 64).wait()


def second_half(dil_ref, own_ref, other_ref, w_ref, bias_ref, out_ref, m_ref, v_ref, ya, yb, o_ref, sem, osem):
    band = lax.axis_index("band")
    half = lax.rem(band, 2)
    bin0 = lax.axis_index("rows") * BINW - 64
    first_u = band * BAND - 32
    c1 = pltpu.make_async_copy(own_ref, m_ref.at[pl.ds(half * 64, 64)], sem.at[0])
    c2 = pltpu.make_async_copy(other_ref, m_ref.at[pl.ds(64 - half * 64, 64)], sem.at[1])
    c1.start()
    c2.start()
    zero = jnp.zeros((PAD, 2 * PC, W2), jnp.bfloat16)
    for y in (ya, yb):
        y[0:PAD] = zero
        y[PAD + R:] = zero
    c1.wait()
    c2.wait()
    bins = lax.broadcasted_iota(jnp.int32, (1, W2), 1) + bin0

    def init(t, carry):
        for s in range(4):
            start(t * 4 + s)
        return carry

    def start(j):
        u = first_u + j
        ui = jnp.clip(u, 0, DIAGS - 1)
        own = pltpu.roll(m_ref[ui], W1 - 64, 1)[:, :W2]
        pi = jnp.clip(DIAGS - u, 0, DIAGS - 1)
        partner = pltpu.roll(m_ref[pi], (W1 - ui) % W1, 1)[:, :W2]
        partner = jnp.where(u > 0, partner, 0.0)
        x = jnp.where(valid_of(u, bins), 0.5 * (own + partner), 0.0)
        v_ref[j] = x
        split_store(ya, j + PAD, jnp.maximum(x, 0.0))

    lax.fori_loop(0, R // 4, init, 0)

    def rows_of(n):
        return 8 * n + 8, 80 - 16 * n

    def out_copy(j):
        return pltpu.make_async_copy(o_ref.at[j], out_ref.at[:, j, :], osem.at[j])

    def done(base, rows):
        for r in range(rows):
            j = base - 32 + r
            o_ref[j] = pltpu.roll(v_ref[j + 32], W2 - 64, 1)[:, :BINW]
            out_copy(j).start()

    blocks(dil_ref, 2, w_ref, bias_ref, v_ref, ya, yb, first_u, bins, rows_of, done)
    for j in range(BAND):
        out_copy(j).wait()


smem = pl.BlockSpec(memory_space=pltpu.SMEM)
vmem = pl.BlockSpec(memory_space=pltpu.VMEM)
hbm = pl.BlockSpec(memory_space=pl.ANY)
LIMIT = 56 * 2 ** 20


def run_gather(features, deleted, emb, conv_weight, conv_bias):
    return pl.pallas_call(
        gather,
        out_shape=[
            jax.ShapeDtypeStruct((FW, 128), jnp.bfloat16),
            jax.ShapeDtypeStruct((4, PC, BAND), jnp.float32),
            jax.ShapeDtypeStruct((4, 192, 192), jnp.bfloat16),
            jax.ShapeDtypeStruct((4, 192, 192), jnp.bfloat16),
            jax.ShapeDtypeStruct((4, PC, 128), jnp.float32),
            jax.ShapeDtypeStruct((4, PC, 128), jnp.float32),
        ],
        in_specs=[vmem] * 5,
        out_specs=[vmem] * 6,
        scratch_shapes=[
            pltpu.VMEM((64, 128), jnp.bfloat16),
            pltpu.VMEM((3, 4, 64, 128), jnp.bfloat16),
            pltpu.VMEM((4, PC, BAND), jnp.float32),
            pltpu.SemaphoreType.DMA((11,)),
            pltpu.SemaphoreType.DMA((3, 4)),
            pltpu.SemaphoreType.DMA((3,)),
            pltpu.SemaphoreType.DMA((4,)),
        ],
        compiler_params=pltpu.CompilerParams(collective_id=0, has_side_effects=True),
        name="gather",
    )(features, deleted.reshape(1, 64), emb, conv_weight, conv_bias.reshape(8, 1, PC))


def run_first(dil, feat, proj, emb, w, bias):
    return pl.pallas_call(
        first_half,
        out_shape=jax.ShapeDtypeStruct((64, PC, W1), jnp.float32),
        in_specs=[
            smem, vmem, vmem, vmem,
            vmem, vmem,
        ],
        out_specs=hbm,
        scratch_shapes=[
            pltpu.VMEM((R, PC, W1), jnp.float32),
            pltpu.VMEM((R + 2 * PAD, 2 * PC, W1), jnp.bfloat16),
            pltpu.VMEM((R + 2 * PAD, 2 * PC, W1), jnp.bfloat16),
            pltpu.VMEM((PC, W1), jnp.float32),
            pltpu.VMEM((PC, FW), jnp.float32),
            pltpu.SemaphoreType.DMA,
        ],
        compiler_params=pltpu.CompilerParams(vmem_limit_bytes=LIMIT),
        name="first_half",
    )(dil, feat, proj, emb, w, bias)


def run_second(dil, own, other, w, bias):
    return pl.pallas_call(
        second_half,
        out_shape=jax.ShapeDtypeStruct((PC, BAND, BINW), jnp.float32),
        in_specs=[
            smem, hbm, hbm,
            vmem, vmem,
        ],
        out_specs=hbm,
        scratch_shapes=[
            pltpu.VMEM((DIAGS, PC, W1), jnp.float32),
            pltpu.VMEM((R, PC, W2), jnp.float32),
            pltpu.VMEM((R + 2 * PAD, 2 * PC, W2), jnp.bfloat16),
            pltpu.VMEM((R + 2 * PAD, 2 * PC, W2), jnp.bfloat16),
            pltpu.VMEM((BAND, PC, BINW), jnp.float32),
            pltpu.SemaphoreType.DMA((2,)),
            pltpu.SemaphoreType.DMA((BAND,)),
        ],
        compiler_params=pltpu.CompilerParams(vmem_limit_bytes=LIMIT),
        name="second_half",
    )(dil, own, other, w, bias)


def body(features, deleted, proj_weight, distance_embed, conv_weight, conv_bias, dilations):
    feat, emb, w_first, w_second, bias_first, bias_second = run_gather(features, deleted, distance_embed, conv_weight, conv_bias)
    mine = run_first(dilations, feat, proj_weight, emb, w_first, bias_first)
    other = lax.ppermute(mine, "band", [(0, 1), (1, 0), (2, 3), (3, 2)])
    return run_second(dilations, mine, other, w_second, bias_second)


def solution(mesh):
    return jax.shard_map(
        body,
        mesh=mesh,
        in_specs=(
            P(("rows", "band"), None),
            P(("rows", "band")),
            P(),
            P(None, "band"),
            P(),
            P(),
            P(),
        ),
        out_specs=P(None, "band", "rows"),
        check_vma=False,
    )
```

```python
import jax
import jax.numpy as jnp
from jax import lax
from jax.experimental import pallas as pl
from jax.experimental.pallas import tpu as pltpu
from jax.sharding import PartitionSpec as P

PC = 32
DIAGS = 128
HALF = 64
BAND = 32
BINW = 256
MAXDIL = 8
BINS = 8192
W1 = 512
W2 = 384
FW = 640
R = 96
PAD = 8
UNROLL = 16
ROWS = 32
MESH = pl.DeviceIdType.MESH


def split_store(y_ref, j, x):
    hi = x.astype(jnp.bfloat16)
    lo = (x - hi.astype(jnp.float32)).astype(jnp.bfloat16)
    y_ref[j, 0:PC, :] = hi
    y_ref[j, PC:2 * PC, :] = lo


def gather_taps(p, k, bias):
    width = p.shape[1]
    parts = [p[64 * b:64 * b + 32] + p[64 * b + 32:64 * b + 64] for b in range(3)]
    return (
        parts[1]
        + pltpu.roll(parts[0], k, 1)
        + pltpu.roll(parts[2], width - k, 1)
        + bias
    )


def valid_of(u, bins):
    low = jnp.maximum(0, HALF - u)
    high = jnp.where((u >= 0) & (u < DIAGS), jnp.minimum(BINS, BINS + HALF - u), 0)
    return (bins >= low) & (bins < high)


def conv(k, weights, bias, src, dst, v_ref, first_u, bins, start, count, n, last):
    width = bins.shape[1]
    cat = 2 if width % 256 else 1

    def group(base, rows):
        for g in range(0, rows, cat):
            stack = [
                jnp.concatenate([src[j - k], src[j], src[j + k]], axis=0)
                for j in [base + g + c + PAD for c in range(cat)]
            ]
            stack = stack[0] if cat == 1 else jnp.concatenate(stack, axis=1)
            p = jnp.dot(weights, stack, preferred_element_type=jnp.float32)
            for c in range(cat):
                j = base + g + c
                branch = gather_taps(p[:, c * width:(c + 1) * width], k, bias)
                branch = jnp.where(valid_of(first_u + j, bins), branch, 0.0)
                if n == 3:
                    last[0](j, v_ref[j] + branch)
                    continue
                if n == 1:
                    branch = v_ref[j] + branch
                    v_ref[j] = branch
                split_store(dst, j + PAD, jnp.maximum(branch, 0.0))

    def step(t, carry):
        group(start + t * UNROLL, UNROLL)
        if n == 3:
            last[1](t)
        return carry

    lax.fori_loop(0, count // UNROLL, step, 0)
    if count % UNROLL:
        group(start + count // UNROLL * UNROLL, count % UNROLL)


def blocks(dil_ref, first, w_ref, bias_ref, v_ref, ya, yb, first_u, bins, rows_of, last):
    for n in range(4):
        src, dst = (ya, yb) if n % 2 == 0 else (yb, ya)
        start, count = rows_of(n)
        bias = jnp.concatenate([bias_ref[first + n]] * (bins.shape[1] // 128), axis=1)
        conv(
            dil_ref[(first + n) // 2], w_ref[first + n], bias, src, dst, v_ref,
            first_u, bins, start, count, n, last,
        )


def trunk(dil_ref, feat_ref, del_ref, proj_ref, emb_ref, cw_ref, cb_ref, out_ref,
          kept, land, emb_land, w_ref, bias_ref, row_s, col_s, v_ref, ya, yb, m_ref, v2_ref, ya2, yb2, o_ref,
          send, recv, esend, erecv, msend, mrecv, osem):
    row = lax.axis_index("rows")
    band = lax.axis_index("band")
    near = [(row, lax.rem(band + d, 4)) for d in range(1, 4)]
    after = [(lax.rem(row + 1, ROWS), d) for d in range(4)]
    before = [(lax.rem(row + ROWS - 1, ROWS), d) for d in range(4)]
    barrier = pltpu.get_barrier_semaphore()
    for r, b in near + after + before:
        pl.semaphore_signal(barrier, inc=1, device_id={"rows": r, "band": b}, device_id_type=MESH)

    same = lax.broadcasted_iota(jnp.int32, (64, 64), 0) == lax.broadcasted_iota(jnp.int32, (64, 64), 1)
    gone = jnp.sum(jnp.where(same, del_ref[...].astype(jnp.float32), 0.0), axis=1, keepdims=True)
    kept[...] = (feat_ref[...].astype(jnp.float32) * (1.0 - gone)).astype(jnp.bfloat16)

    pl.semaphore_wait(barrier, 11)
    copies = []

    def send_to(r, b, slot, index):
        copies.append(pltpu.make_async_remote_copy(
            kept, land.at[pl.ds(256 * slot + 64 * band, 64)], send.at[index], recv.at[slot, band],
            device_id={"rows": r, "band": b}, device_id_type=MESH))

    for d, (r, b) in enumerate(near):
        send_to(r, b, 1, d)
    for d, (r, b) in enumerate(after):
        send_to(r, b, 0, 3 + d)
    for d, (r, b) in enumerate(before):
        send_to(r, b, 2, 7 + d)
    for d, (r, b) in enumerate(near):
        copies.append(pltpu.make_async_remote_copy(
            emb_ref, emb_land.at[band], esend.at[d], erecv.at[band],
            device_id={"rows": r, "band": b}, device_id_type=MESH))
    for copy in copies:
        copy.start()
    land[pl.ds(256 + 64 * band, 64), :] = kept[...]
    emb_land[band] = emb_ref[...]

    square = lax.broadcasted_iota(jnp.int32, (PC, PC), 0) == lax.broadcasted_iota(jnp.int32, (PC, PC), 1)

    def weights(n, carry):
        for b in range(3):
            t = [cw_ref[n, 3 * a + b] for a in range(3)]
            wide = jnp.concatenate([t[0], t[0], t[1], t[1], t[2], t[2]], axis=1)
            high = wide.astype(jnp.bfloat16)
            w_ref[n, 64 * b:64 * b + 32, :] = high
            w_ref[n, 64 * b + 32:64 * b + 64, :] = (wide - high.astype(jnp.float32)).astype(jnp.bfloat16)
        column = jnp.sum(jnp.where(square, cb_ref[n], 0.0), axis=1, keepdims=True)
        bias_ref[n] = jnp.broadcast_to(column, (PC, 128))
        return carry

    lax.fori_loop(0, 8, weights, 0)
    for y, width in ((ya, W1), (yb, W1), (ya2, W2), (yb2, W2)):
        zero = jnp.zeros((PAD, 2 * PC, width), jnp.bfloat16)
        y[0:PAD] = zero
        y[PAD + R:] = zero

    def arrived(buf, sem):
        pltpu.make_async_copy(buf, buf, sem).wait()

    for d in range(1, 4):
        b = lax.rem(band + d, 4)
        arrived(land.at[pl.ds(256 + 64 * b, 64)], recv.at[1, b])
        arrived(emb_land.at[b], erecv.at[b])
    for d in range(4):
        arrived(land.at[pl.ds(64 * d, 64)], recv.at[0, d])
        arrived(land.at[pl.ds(512 + 64 * d, 64)], recv.at[2, d])

    half = lax.rem(band, 2)
    pair = lax.div(band, 2)
    first_u = half * 32
    skip = 128 - 128 * pair
    bin0 = row * BINW - 160 + 64 * pair
    projected = lax.dot_general(
        proj_ref[...], land[pl.ds(32 + 64 * pair, FW), :], (((0,), (1,)), ((), ())),
        preferred_element_type=jnp.float32,
    )
    row_s[...] = projected[:PC, 64:64 + W1]
    col_s[...] = projected[PC:]
    bins = lax.broadcasted_iota(jnp.int32, (1, W1), 1) + bin0
    lanes = lax.broadcasted_iota(jnp.int32, (PC, BAND), 1)

    def start_rows(t, carry):
        for s in range(8):
            j = t * 8 + s
            u = first_u + j
            col = pltpu.roll(col_s[...], FW - u, 1)[:, :W1]
            emb = jnp.where(lanes == lax.rem(u, BAND), emb_land[lax.div(u, BAND)], 0.0)
            x = jnp.maximum(row_s[...] + col + jnp.sum(emb, axis=1, keepdims=True), 0.0)
            x = jnp.where(valid_of(u, bins), x, 0.0)
            v_ref[j] = x
            split_store(ya, j + PAD, x)
        return carry

    lax.fori_loop(0, R // 8, start_rows, 0)

    def swap(index, base):
        rows = m_ref.at[pl.ds(base, 16)]
        return pltpu.make_async_remote_copy(
            rows, rows, msend.at[index], mrecv.at[index],
            device_id={"rows": row, "band": band + 1 - 2 * half}, device_id_type=MESH)

    def keep(j, value):
        m_ref[first_u + j] = value

    def keep_done(t):
        swap(t, 64 * half + 16 * t).start()

    blocks(dil_ref, 0, w_ref, bias_ref, v_ref, ya, yb, first_u, bins,
           lambda n: (half * (8 * n + 8), 88 - 8 * n), (keep, keep_done))
    for t in range(4):
        swap(t, 64 * half + 16 * t).wait_send()
        swap(t, 64 - 64 * half + 16 * t).wait_recv()

    u2 = band * BAND - 32
    bins2 = lax.broadcasted_iota(jnp.int32, (1, W2), 1) + (bin0 + skip)

    def mirror_rows(t, carry):
        for s in range(8):
            j = t * 8 + s
            u = u2 + j
            ui = jnp.clip(u, 0, DIAGS - 1)
            own = m_ref[ui, :, pl.ds(pl.multiple_of(skip, 128), W2)]
            partner = m_ref[jnp.clip(DIAGS - u, 0, DIAGS - 1)]
            partner = pltpu.roll(partner, lax.rem(W1 + HALF - skip - ui + W1, W1), 1)[:, :W2]
            partner = jnp.where(u > 0, partner, 0.0)
            x = jnp.where(valid_of(u, bins2), 0.5 * (own + partner), 0.0)
            v2_ref[j] = x
            split_store(ya2, j + PAD, jnp.maximum(x, 0.0))
        return carry

    lax.fori_loop(0, R // 8, mirror_rows, 0)

    shift = W2 - 32 - 64 * pair

    def emit(j, value):
        o_ref[j - 32] = pltpu.roll(value, shift, 1)[:, :BINW]

    def out_copy(j):
        return pltpu.make_async_copy(o_ref.at[j], out_ref.at[:, j, :], osem.at[j])

    def emit_done(t):
        for r in range(16):
            out_copy(16 * t + r).start()

    blocks(dil_ref, 4, w_ref, bias_ref, v2_ref, ya2, yb2, u2, bins2,
           lambda n: (8 * n + 8, 80 - 16 * n), (emit, emit_done))
    for j in range(BAND):
        out_copy(j).wait()
    for copy in copies:
        copy.wait_send()


smem = pl.BlockSpec(memory_space=pltpu.SMEM)
vmem = pl.BlockSpec(memory_space=pltpu.VMEM)
hbm = pl.BlockSpec(memory_space=pl.ANY)
f32 = jnp.float32
bf16 = jnp.bfloat16


def body(features, deleted, proj_weight, distance_embed, conv_weight, conv_bias, dilations):
    dma = pltpu.SemaphoreType.DMA
    return pl.pallas_call(
        trunk,
        out_shape=jax.ShapeDtypeStruct((PC, BAND, BINW), f32),
        in_specs=[smem] + [vmem] * 6,
        out_specs=hbm,
        scratch_shapes=[
            pltpu.VMEM((64, 128), bf16),
            pltpu.VMEM((768, 128), bf16),
            pltpu.VMEM((4, PC, BAND), f32),
            pltpu.VMEM((8, 192, 192), bf16),
            pltpu.VMEM((8, PC, 128), f32),
            pltpu.VMEM((PC, W1), f32),
            pltpu.VMEM((PC, FW), f32),
            pltpu.VMEM((R, PC, W1), f32),
            pltpu.VMEM((R + 2 * PAD, 2 * PC, W1), bf16),
            pltpu.VMEM((R + 2 * PAD, 2 * PC, W1), bf16),
            pltpu.VMEM((DIAGS, PC, W1), f32),
            pltpu.VMEM((R, PC, W2), f32),
            pltpu.VMEM((R + 2 * PAD, 2 * PC, W2), bf16),
            pltpu.VMEM((R + 2 * PAD, 2 * PC, W2), bf16),
            pltpu.VMEM((BAND, PC, BINW), f32),
            dma((11,)), dma((3, 4)), dma((3,)), dma((4,)), dma((4,)), dma((4,)), dma((BAND,)),
        ],
        compiler_params=pltpu.CompilerParams(
            collective_id=0, has_side_effects=True, vmem_limit_bytes=58 * 2 ** 20),
        name="trunk",
    )(dilations, features, deleted.reshape(1, 64), proj_weight, distance_embed, conv_weight, conv_bias.reshape(8, 1, PC))


def solution(mesh):
    return jax.shard_map(
        body,
        mesh=mesh,
        in_specs=(
            P(("rows", "band"), None),
            P(("rows", "band")),
            P(),
            P(None, "band"),
            P(),
            P(),
            P(),
        ),
        out_specs=P(None, "band", "rows"),
        check_vma=False,
    )
```

```python
import jax
import jax.numpy as jnp
from jax import lax
from jax.experimental import pallas as pl
from jax.experimental.pallas import tpu as pltpu
from jax.sharding import PartitionSpec as P

PC = 32
DIAGS = 128
HALF = 64
BAND = 32
BINW = 256
MAXDIL = 8
BINS = 8192
W1 = 512
W2 = 384
FW = 640
HALO = 8
R1 = 80
R2 = 72
ROWS = 32
MESH = pl.DeviceIdType.MESH


def split_store(y_ref, j, x):
    hi = x.astype(jnp.bfloat16)
    lo = (x - hi.astype(jnp.float32)).astype(jnp.bfloat16)
    y_ref[j, 0:PC, :] = hi
    y_ref[j, PC:2 * PC, :] = lo


def gather_taps(p, k, bias):
    width = p.shape[1]
    parts = [p[64 * b:64 * b + 32] + p[64 * b + 32:64 * b + 64] for b in range(3)]
    return (
        parts[1]
        + pltpu.roll(parts[0], k, 1)
        + pltpu.roll(parts[2], width - k, 1)
        + bias
    )


def valid_of(u, bins):
    low = jnp.maximum(0, HALF - u)
    high = jnp.where((u >= 0) & (u < DIAGS), jnp.minimum(BINS, BINS + HALF - u), 0)
    return (bins >= low) & (bins < high)


def conv_rows(ctx, base, count, sink):
    k, weights, bias, src, u0, bins = ctx
    width = bins.shape[1]
    cat = 2 if width % 256 else 1
    for g in range(0, count, cat):
        stack = [
            jnp.concatenate([src[q - k], src[q], src[q + k]], axis=0)
            for q in [base + g + c for c in range(cat)]
        ]
        stack = stack[0] if cat == 1 else jnp.concatenate(stack, axis=1)
        p = jnp.dot(weights, stack, preferred_element_type=jnp.float32)
        for c in range(cat):
            q = base + g + c
            branch = gather_taps(p[:, c * width:(c + 1) * width], k, bias)
            sink(q, jnp.where(valid_of(u0 + q, bins), branch, 0.0))


def trunk(dil_ref, feat_ref, del_ref, proj_ref, emb_ref, cw_ref, cb_ref, out_ref,
          kept, land, emb_land, w_ref, bias_ref, row_s, col_s, v_ref, ya, yb, m_ref, v2_ref, ya2, yb2, o_ref, halo1, halo2,
          send, recv, esend, erecv, msend, mrecv, hsend, hrecv, osem):
    row = lax.axis_index("rows")
    band = lax.axis_index("band")
    near = [(row, lax.rem(band + d, 4)) for d in range(1, 4)]
    after = [(lax.rem(row + 1, ROWS), d) for d in range(4)]
    before = [(lax.rem(row + ROWS - 1, ROWS), d) for d in range(4)]
    barrier = pltpu.get_barrier_semaphore()
    for r, b in near + after + before:
        pl.semaphore_signal(barrier, inc=1, device_id={"rows": r, "band": b}, device_id_type=MESH)

    same = lax.broadcasted_iota(jnp.int32, (64, 64), 0) == lax.broadcasted_iota(jnp.int32, (64, 64), 1)
    gone = jnp.sum(jnp.where(same, del_ref[...].astype(jnp.float32), 0.0), axis=1, keepdims=True)
    kept[...] = (feat_ref[...].astype(jnp.float32) * (1.0 - gone)).astype(jnp.bfloat16)

    pl.semaphore_wait(barrier, 11)
    copies = []

    def send_to(r, b, slot, index):
        copies.append(pltpu.make_async_remote_copy(
            kept, land.at[pl.ds(256 * slot + 64 * band, 64)], send.at[index], recv.at[slot, band],
            device_id={"rows": r, "band": b}, device_id_type=MESH))

    for d, (r, b) in enumerate(near):
        send_to(r, b, 1, d)
    for d, (r, b) in enumerate(after):
        send_to(r, b, 0, 3 + d)
    for d, (r, b) in enumerate(before):
        send_to(r, b, 2, 7 + d)
    for d, (r, b) in enumerate(near):
        copies.append(pltpu.make_async_remote_copy(
            emb_ref, emb_land.at[band], esend.at[d], erecv.at[band],
            device_id={"rows": r, "band": b}, device_id_type=MESH))
    for copy in copies:
        copy.start()
    land[pl.ds(256 + 64 * band, 64), :] = kept[...]
    emb_land[band] = emb_ref[...]

    square = lax.broadcasted_iota(jnp.int32, (PC, PC), 0) == lax.broadcasted_iota(jnp.int32, (PC, PC), 1)

    def weights(n, carry):
        for b in range(3):
            t = [cw_ref[n, 3 * a + b] for a in range(3)]
            wide = jnp.concatenate([t[0], t[0], t[1], t[1], t[2], t[2]], axis=1)
            high = wide.astype(jnp.bfloat16)
            w_ref[n, 64 * b:64 * b + 32, :] = high
            w_ref[n, 64 * b + 32:64 * b + 64, :] = (wide - high.astype(jnp.float32)).astype(jnp.bfloat16)
        column = jnp.sum(jnp.where(square, cb_ref[n], 0.0), axis=1, keepdims=True)
        bias_ref[n] = jnp.broadcast_to(column, (PC, 128))
        return carry

    lax.fori_loop(0, 8, weights, 0)
    zero = jnp.zeros((HALO, 2 * PC, W1), jnp.bfloat16)
    for y in (ya, yb):
        y[0:HALO] = zero
        y[R1 - HALO:] = zero

    def arrived(buf, sem):
        pltpu.make_async_copy(buf, buf, sem).wait()

    for d in range(1, 4):
        b = lax.rem(band + d, 4)
        arrived(land.at[pl.ds(256 + 64 * b, 64)], recv.at[1, b])
        arrived(emb_land.at[b], erecv.at[b])
    for d in range(4):
        arrived(land.at[pl.ds(64 * d, 64)], recv.at[0, d])
        arrived(land.at[pl.ds(512 + 64 * d, 64)], recv.at[2, d])

    half = lax.rem(band, 2)
    pair = lax.div(band, 2)
    other = band + 1 - 2 * half
    u0 = 64 * half - HALO
    skip = 128 - 128 * pair
    bin0 = row * BINW - 160 + 64 * pair
    projected = lax.dot_general(
        proj_ref[...], land[pl.ds(32 + 64 * pair, FW), :], (((1,), (1,)), ((), ())),
        preferred_element_type=jnp.float32,
    )
    row_s[...] = projected[:PC, 64:64 + W1]
    col_s[...] = projected[PC:]
    bins = lax.broadcasted_iota(jnp.int32, (1, W1), 1) + bin0
    lanes = lax.broadcasted_iota(jnp.int32, (PC, BAND), 1)

    def start_rows(t, carry):
        for s in range(24):
            q = HALO - HALO * half + t * 24 + s
            u = u0 + q
            col = pltpu.roll(col_s[...], FW - u, 1)[:, :W1]
            emb = jnp.where(lanes == lax.rem(u, BAND), emb_land[lax.div(u, BAND)], 0.0)
            x = jnp.maximum(row_s[...] + col + jnp.sum(emb, axis=1, keepdims=True), 0.0)
            x = jnp.where(valid_of(u, bins), x, 0.0)
            v_ref[q] = x
            split_store(ya, q, x)
        return carry

    lax.fori_loop(0, 3, start_rows, 0)

    def context(n, src, u0, bins):
        bias = jnp.concatenate([bias_ref[n]] * (bins.shape[1] // 128), axis=1)
        return dil_ref[n // 2], w_ref[n], bias, src, u0, bins

    def branch_to(v, dst, residual):
        def sink(q, value):
            if residual:
                value = v[q] + value
                v[q] = value
            split_store(dst, q, jnp.maximum(value, 0.0))
        return sink

    def to_other(src, dst, ssem, rsem):
        return pltpu.make_async_remote_copy(
            src, dst, ssem, rsem, device_id={"rows": row, "band": other}, device_id_type=MESH)

    def edge1(n, dst):
        edge = dst.at[pl.ds(64 - 56 * half, HALO)]
        return to_other(edge, halo1.at[n], hsend.at[n], hrecv.at[n])

    for n in range(3):
        src, dst = (ya, yb) if n % 2 == 0 else (yb, ya)
        if n:
            edge1(n - 1, src).wait()
            src[pl.ds(72 - 72 * half, HALO)] = halo1[n - 1]
        ctx = context(n, src, u0, bins)
        sink = branch_to(v_ref, dst, n == 1)

        def step(t, carry, n=n, dst=dst, ctx=ctx, sink=sink):
            conv_rows(ctx, HALO + half * (32 * t) + (1 - half) * (32 - 32 * t), 32, sink)

            @pl.when(t == 0)
            def _():
                edge1(n, dst).start()

            return carry

        lax.fori_loop(0, 2, step, 0)

    edge1(2, yb).wait()
    yb[pl.ds(72 - 72 * half, HALO)] = halo1[2]
    ctx3 = context(3, yb, u0, bins)

    def swap(t, core, count):
        at = 64 * core + (16 * t if count == 16 else 32) * pair + (48 - 16 * t if count == 16 else 20) * (1 - pair)
        rows = m_ref.at[pl.ds(at, count)]
        return to_other(rows, rows, msend.at[t], mrecv.at[t])

    def keep(q, value):
        m_ref[u0 + q] = v_ref[q] + value

    def last_step(t, carry):
        conv_rows(ctx3, HALO + 16 * t * pair + (48 - 16 * t) * (1 - pair), 16, keep)

        @pl.when(t < 2)
        def _():
            swap(t, half, 16).start()

        @pl.when(t == 2)
        def _():
            swap(2, half, 12).start()

        return carry

    lax.fori_loop(0, 4, last_step, 0)
    for t in range(3):
        count = 16 if t < 2 else 12
        swap(t, half, count).wait_send()
        swap(t, 1 - half, count).wait_recv()

    u2 = band * BAND - 32 + 24 * half
    bins2 = lax.broadcasted_iota(jnp.int32, (1, W2), 1) + (bin0 + skip)

    def mirror_rows(t, carry):
        for s in range(24):
            q = t * 24 + s
            u = u2 + q
            ui = jnp.clip(u, 0, DIAGS - 1)
            own = m_ref[ui, :, pl.ds(pl.multiple_of(skip, 128), W2)]
            partner = m_ref[jnp.clip(DIAGS - u, 0, DIAGS - 1)]
            partner = pltpu.roll(partner, lax.rem(W1 + HALF - skip - ui + W1, W1), 1)[:, :W2]
            partner = jnp.where(u > 0, partner, 0.0)
            x = jnp.where(valid_of(u, bins2), 0.5 * (own + partner), 0.0)
            v2_ref[q] = x
            split_store(ya2, q, jnp.maximum(x, 0.0))
        return carry

    lax.fori_loop(0, 3, mirror_rows, 0)

    def edge2(n, dst):
        edge = dst.at[pl.ds(56 - 48 * half, HALO)]
        return to_other(edge, halo2.at[n], hsend.at[3 + n], hrecv.at[3 + n])

    for n in range(3):
        src, dst = (ya2, yb2) if n % 2 == 0 else (yb2, ya2)
        if n:
            edge2(n - 1, src).wait()
            src[pl.ds(64 - 64 * half, HALO)] = halo2[n - 1]
        ctx = context(4 + n, src, u2, bins2)
        sink = branch_to(v2_ref, dst, n == 1)
        conv_rows(ctx, 32 - 24 * half, 32, sink)
        edge2(n, dst).start()
        conv_rows(ctx, (8 + 8 * n) * (1 - half) + 40 * half, 24 - 8 * n, sink)
    edge2(2, yb2).wait()
    yb2[pl.ds(64 - 64 * half, HALO)] = halo2[2]

    shift = W2 - 32 - 64 * pair
    first = 32 - 24 * half
    ctx7 = context(7, yb2, u2, bins2)

    def emit(q, value):
        o_ref[q - first] = pltpu.roll(v2_ref[q] + value, shift, 1)[:, :BINW]

    def out_copy(j):
        return pltpu.make_async_copy(o_ref.at[j], out_ref.at[:, j, :], osem.at[j])

    for t in range(2):
        conv_rows(ctx7, first + 16 * t, 16, emit)
        for r in range(16):
            out_copy(16 * t + r).start()
    for j in range(BAND):
        out_copy(j).wait()
    for copy in copies:
        copy.wait_send()


smem = pl.BlockSpec(memory_space=pltpu.SMEM)
vmem = pl.BlockSpec(memory_space=pltpu.VMEM)
hbm = pl.BlockSpec(memory_space=pl.ANY)
f32 = jnp.float32
bf16 = jnp.bfloat16


def body(features, deleted, proj_weight, distance_embed, conv_weight, conv_bias, dilations):
    dma = pltpu.SemaphoreType.DMA
    return pl.pallas_call(
        trunk,
        out_shape=jax.ShapeDtypeStruct((PC, BAND, BINW), f32),
        in_specs=[smem] + [vmem] * 6,
        out_specs=hbm,
        scratch_shapes=[
            pltpu.VMEM((64, 128), bf16),
            pltpu.VMEM((768, 128), bf16),
            pltpu.VMEM((4, PC, BAND), f32),
            pltpu.VMEM((8, 192, 192), bf16),
            pltpu.VMEM((8, PC, 128), f32),
            pltpu.VMEM((PC, W1), f32),
            pltpu.VMEM((PC, FW), f32),
            pltpu.VMEM((R1, PC, W1), f32),
            pltpu.VMEM((R1, 2 * PC, W1), bf16),
            pltpu.VMEM((R1, 2 * PC, W1), bf16),
            pltpu.VMEM((DIAGS, PC, W1), f32),
            pltpu.VMEM((R2, PC, W2), f32),
            pltpu.VMEM((R2, 2 * PC, W2), bf16),
            pltpu.VMEM((R2, 2 * PC, W2), bf16),
            pltpu.VMEM((BAND, PC, BINW), f32),
            pltpu.VMEM((3, HALO, 2 * PC, W1), bf16),
            pltpu.VMEM((3, HALO, 2 * PC, W2), bf16),
            dma((11,)), dma((3, 4)), dma((3,)), dma((4,)), dma((3,)), dma((3,)), dma((6,)), dma((6,)), dma((BAND,)),
        ],
        compiler_params=pltpu.CompilerParams(
            collective_id=0, has_side_effects=True, vmem_limit_bytes=58 * 2 ** 20),
        name="trunk",
    )(dilations, features, deleted.reshape(1, 64), proj_weight.T, distance_embed, conv_weight, conv_bias.reshape(8, 1, PC))


def solution(mesh):
    return jax.shard_map(
        body,
        mesh=mesh,
        in_specs=(
            P(("rows", "band"), None),
            P(("rows", "band")),
            P(),
            P(None, "band"),
            P(),
            P(),
            P(),
        ),
        out_specs=P(None, "band", "rows"),
        check_vma=False,
    )
```

```python
import jax
import jax.numpy as jnp
from jax import lax
from jax.experimental import pallas as pl
from jax.experimental.pallas import tpu as pltpu
from jax.sharding import PartitionSpec as P

PC = 32
DIAGS = 128
HALF = 64
BAND = 32
BINW = 256
MAXDIL = 8
BINS = 8192
W1 = 512
W2 = 384
FW = 512
HALO = 8
R1 = 80
R2 = 72
ROWS = 32
MESH = pl.DeviceIdType.MESH


def split_store(y_ref, j, x):
    hi = x.astype(jnp.bfloat16)
    lo = (x - hi.astype(jnp.float32)).astype(jnp.bfloat16)
    y_ref[j, 0:PC, :] = hi
    y_ref[j, PC:2 * PC, :] = lo


def gather_taps(p, k, bias):
    width = p.shape[1]
    parts = [p[64 * b:64 * b + 32] + p[64 * b + 32:64 * b + 64] for b in range(3)]
    return (
        parts[1]
        + pltpu.roll(parts[0], k, 1)
        + pltpu.roll(parts[2], width - k, 1)
        + bias
    )


def valid_of(u, bins):
    low = jnp.maximum(0, HALF - u)
    high = jnp.where((u >= 0) & (u < DIAGS), jnp.minimum(BINS, BINS + HALF - u), 0)
    return (bins >= low) & (bins < high)


def conv_rows(ctx, base, count, sink):
    k, weights, bias, src, u0, bins = ctx
    width = bins.shape[1]
    cat = 2 if width % 256 else 1
    for g in range(0, count, cat):
        stack = [
            jnp.concatenate([src[q - k], src[q], src[q + k]], axis=0)
            for q in [base + g + c for c in range(cat)]
        ]
        stack = stack[0] if cat == 1 else jnp.concatenate(stack, axis=1)
        p = jnp.dot(weights, stack, preferred_element_type=jnp.float32)
        for c in range(cat):
            q = base + g + c
            branch = gather_taps(p[:, c * width:(c + 1) * width], k, bias)
            sink(q, jnp.where(valid_of(u0 + q, bins), branch, 0.0))


def trunk(dil_ref, feat_ref, del_ref, proj_ref, emb_ref, cw_hbm, cb_ref, out_ref,
          kept, land, emb_land, cw_ref, w_ref, bias_ref, row_s, col_s, v_ref, ya, yb, m_ref, v2_ref, ya2, yb2, o_ref, halo1, halo2,
          cw_sem, send, recv, esend, erecv, msend, mrecv, hsend, hrecv, osem):
    row = lax.axis_index("rows")
    band = lax.axis_index("band")
    weights_in = pltpu.make_async_copy(cw_hbm, cw_ref, cw_sem)
    weights_in.start()
    near = [(row, lax.rem(band + d, 4)) for d in range(1, 4)]
    upper = lax.div(band, 2)
    far_row = jnp.clip(row + 2 * upper - 1, 0, ROWS - 1)
    far = far_row != row
    barrier = pltpu.get_barrier_semaphore()

    def greet(r, b):
        pl.semaphore_signal(barrier, inc=1, device_id={"rows": r, "band": b}, device_id_type=MESH)

    for r, b in near:
        greet(r, b)

    @pl.when(row > 0)
    def _():
        greet(row - 1, 2)
        greet(row - 1, 3)

    @pl.when(row < ROWS - 1)
    def _():
        greet(row + 1, 0)
        greet(row + 1, 1)

    same = lax.broadcasted_iota(jnp.int32, (64, 64), 0) == lax.broadcasted_iota(jnp.int32, (64, 64), 1)
    gone = jnp.sum(jnp.where(same, del_ref[...].astype(jnp.float32), 0.0), axis=1, keepdims=True)
    kept[...] = (feat_ref[...].astype(jnp.float32) * (1.0 - gone)).astype(jnp.bfloat16)

    pl.semaphore_wait(barrier, jnp.where(far, 7, 3))

    def slot(i):
        return land.at[pl.ds(64 * i, 64)]

    def send_to(r, b, to, index):
        return pltpu.make_async_remote_copy(
            kept, slot(to), send.at[index], recv.at[to],
            device_id={"rows": r, "band": b}, device_id_type=MESH)

    def send_far(d):
        return send_to(far_row, d, lax.rem(band + 6, 8), 3 + d)

    def send_emb(d, r, b):
        return pltpu.make_async_remote_copy(
            emb_ref, emb_land.at[band], esend.at[d], erecv.at[band],
            device_id={"rows": r, "band": b}, device_id_type=MESH)

    @pl.when(far)
    def _():
        for d in range(4):
            send_far(d).start()

    for d, (r, b) in enumerate(near):
        send_to(r, b, 2 + band, d).start()
    for d, (r, b) in enumerate(near):
        send_emb(d, r, b).start()
    land[pl.ds(128 + 64 * band, 64), :] = kept[...]
    emb_land[band] = emb_ref[...]
    none = jnp.zeros((128, 128), jnp.bfloat16)

    @pl.when(row == 0)
    def _():
        land[0:128] = none

    @pl.when(row == ROWS - 1)
    def _():
        land[384:512] = none

    square = lax.broadcasted_iota(jnp.int32, (PC, PC), 0) == lax.broadcasted_iota(jnp.int32, (PC, PC), 1)

    def weights(n, carry):
        for b in range(3):
            t = [cw_ref[n, 3 * a + b] for a in range(3)]
            wide = jnp.concatenate([t[0], t[0], t[1], t[1], t[2], t[2]], axis=1)
            high = wide.astype(jnp.bfloat16)
            w_ref[n, 64 * b:64 * b + 32, :] = high
            w_ref[n, 64 * b + 32:64 * b + 64, :] = (wide - high.astype(jnp.float32)).astype(jnp.bfloat16)
        column = jnp.sum(jnp.where(square, cb_ref[n], 0.0), axis=1, keepdims=True)
        bias_ref[n] = jnp.broadcast_to(column, (PC, 128))
        return carry

    weights_in.wait()
    lax.fori_loop(0, 8, weights, 0)
    zero = jnp.zeros((HALO, 2 * PC, W1), jnp.bfloat16)
    for y in (ya, yb):
        y[0:HALO] = zero
        y[R1 - HALO:] = zero

    def arrived(buf, sem):
        pltpu.make_async_copy(buf, buf, sem).wait()

    for d in range(1, 4):
        b = lax.rem(band + d, 4)
        arrived(slot(2 + b), recv.at[2 + b])
        arrived(emb_land.at[b], erecv.at[b])

    @pl.when(row > 0)
    def _():
        for i in (0, 1):
            arrived(slot(i), recv.at[i])

    @pl.when(row < ROWS - 1)
    def _():
        for i in (6, 7):
            arrived(slot(i), recv.at[i])

    half = lax.rem(band, 2)
    pair = lax.div(band, 2)
    other = band + 1 - 2 * half
    u0 = 64 * half - HALO
    skip = 128 - 128 * pair
    bin0 = row * BINW - 160 + 64 * pair
    projected = lax.dot_general(
        proj_ref[...], land[...], (((1,), (1,)), ((), ())), preferred_element_type=jnp.float32
    )
    row_s[...] = pltpu.roll(projected[:PC], 32 + (W1 - 64) * pair, 1)
    col_s[...] = projected[PC:]
    bins = lax.broadcasted_iota(jnp.int32, (1, W1), 1) + bin0
    lanes = lax.broadcasted_iota(jnp.int32, (PC, BAND), 1)

    def start_rows(t, carry):
        for s in range(24):
            q = HALO - HALO * half + t * 24 + s
            u = u0 + q
            col = pltpu.roll(col_s[...], lax.rem(2 * W1 + 96 - 64 * pair - u, W1), 1)
            emb = jnp.where(lanes == lax.rem(u, BAND), emb_land[lax.div(u, BAND)], 0.0)
            x = jnp.maximum(row_s[...] + col + jnp.sum(emb, axis=1, keepdims=True), 0.0)
            x = jnp.where(valid_of(u, bins), x, 0.0)
            v_ref[q] = x
            split_store(ya, q, x)
        return carry

    lax.fori_loop(0, 3, start_rows, 0)

    def context(n, src, u0, bins):
        bias = jnp.concatenate([bias_ref[n]] * (bins.shape[1] // 128), axis=1)
        return dil_ref[n // 2], w_ref[n], bias, src, u0, bins

    def branch_to(v, dst, residual):
        def sink(q, value):
            if residual:
                value = v[q] + value
                v[q] = value
            split_store(dst, q, jnp.maximum(value, 0.0))
        return sink

    def to_other(src, dst, ssem, rsem):
        return pltpu.make_async_remote_copy(
            src, dst, ssem, rsem, device_id={"rows": row, "band": other}, device_id_type=MESH)

    def edge1(n, dst):
        edge = dst.at[pl.ds(64 - 56 * half, HALO)]
        return to_other(edge, halo1.at[n], hsend.at[n], hrecv.at[n])

    for n in range(3):
        src, dst = (ya, yb) if n % 2 == 0 else (yb, ya)
        if n:
            edge1(n - 1, src).wait()
            src[pl.ds(72 - 72 * half, HALO)] = halo1[n - 1]
        ctx = context(n, src, u0, bins)
        sink = branch_to(v_ref, dst, n == 1)

        def step(t, carry, n=n, dst=dst, ctx=ctx, sink=sink):
            conv_rows(ctx, HALO + half * (32 * t) + (1 - half) * (32 - 32 * t), 32, sink)

            @pl.when(t == 0)
            def _():
                edge1(n, dst).start()

            return carry

        lax.fori_loop(0, 2, step, 0)

    edge1(2, yb).wait()
    yb[pl.ds(72 - 72 * half, HALO)] = halo1[2]
    ctx3 = context(3, yb, u0, bins)

    def swap(t, core, count):
        at = 64 * core + (16 * t if count == 16 else 32) * pair + (48 - 16 * t if count == 16 else 20) * (1 - pair)
        rows = m_ref.at[pl.ds(at, count)]
        return to_other(rows, rows, msend.at[t], mrecv.at[t])

    def keep(q, value):
        m_ref[u0 + q] = v_ref[q] + value

    def last_step(t, carry):
        conv_rows(ctx3, HALO + 16 * t * pair + (48 - 16 * t) * (1 - pair), 16, keep)

        @pl.when(t < 2)
        def _():
            swap(t, half, 16).start()

        @pl.when(t == 2)
        def _():
            swap(2, half, 12).start()

        return carry

    lax.fori_loop(0, 4, last_step, 0)
    u2 = band * BAND - 32 + 24 * half
    bins2 = lax.broadcasted_iota(jnp.int32, (1, W2), 1) + (bin0 + skip)

    def mirror_rows(start):
        for s in range(8):
            q = start + s
            u = u2 + q
            ui = jnp.clip(u, 0, DIAGS - 1)
            own = m_ref[ui, :, pl.ds(pl.multiple_of(skip, 128), W2)]
            partner = m_ref[jnp.clip(DIAGS - u, 0, DIAGS - 1)]
            partner = pltpu.roll(partner, lax.rem(W1 + HALF - skip - ui + W1, W1), 1)[:, :W2]
            partner = jnp.where(u > 0, partner, 0.0)
            x = jnp.where(valid_of(u, bins2), 0.5 * (own + partner), 0.0)
            v2_ref[q] = x
            split_store(ya2, q, jnp.maximum(x, 0.0))

    ready = (((24, 32), (32, 40), (40, 48)), ((8, 16), (16, 24), (48, 56), (56, 64)), ((0, 0), (64, 8)))
    for t in range(3):
        swap(t, 1 - half, 16 if t < 2 else 12).wait_recv()
        for low, high in ready[t]:
            mirror_rows(low + (high - low) * half)
    for t in range(3):
        swap(t, half, 16 if t < 2 else 12).wait_send()

    def edge2(n, dst):
        edge = dst.at[pl.ds(56 - 48 * half, HALO)]
        return to_other(edge, halo2.at[n], hsend.at[3 + n], hrecv.at[3 + n])

    def land2(n, y):
        edge2(n, y).wait()
        y[pl.ds(64 - 64 * half, HALO)] = halo2[n]

    def rows2(ctx, low, high, count, sink):
        conv_rows(ctx, low + (high - low) * half, count, sink)

    ctx, sink = context(4, ya2, u2, bins2), branch_to(v2_ref, yb2, False)
    rows2(ctx, 40, 8, 24, sink)
    edge2(0, yb2).start()
    rows2(ctx, 8, 32, 32, sink)
    ctx, sink = context(5, yb2, u2, bins2), branch_to(v2_ref, ya2, True)
    rows2(ctx, 16, 24, 32, sink)
    land2(0, yb2)
    rows2(ctx, 48, 8, 16, sink)
    edge2(1, ya2).start()
    ctx, sink = context(6, ya2, u2, bins2), branch_to(v2_ref, yb2, False)
    rows2(ctx, 24, 24, 24, sink)
    land2(1, ya2)
    rows2(ctx, 48, 8, 16, sink)
    edge2(2, yb2).start()

    shift = W2 - 32 - 64 * pair
    first = 32 - 24 * half
    ctx7 = context(7, yb2, u2, bins2)

    def emit(q, value):
        o_ref[q - first] = pltpu.roll(v2_ref[q] + value, shift, 1)[:, :BINW]

    def out_copy(j):
        return pltpu.make_async_copy(o_ref.at[j], out_ref.at[:, j, :], osem.at[j])

    def finish(low, high, count):
        rows2(ctx7, low, high, count, emit)
        for r in range(count):
            out_copy(low + (high - low) * half - first + r).start()

    finish(32, 16, 24)
    land2(2, yb2)
    finish(56, 8, 8)
    for j in range(BAND):
        out_copy(j).wait()
    for d, (r, b) in enumerate(near):
        send_to(r, b, 2 + band, d).wait_send()
        send_emb(d, r, b).wait_send()

    @pl.when(far)
    def _():
        for d in range(4):
            send_far(d).wait_send()


smem = pl.BlockSpec(memory_space=pltpu.SMEM)
vmem = pl.BlockSpec(memory_space=pltpu.VMEM)
hbm = pl.BlockSpec(memory_space=pl.ANY)
f32 = jnp.float32
bf16 = jnp.bfloat16


def body(features, deleted, proj_weight, distance_embed, conv_weight, conv_bias, dilations):
    dma = pltpu.SemaphoreType.DMA
    return pl.pallas_call(
        trunk,
        out_shape=jax.ShapeDtypeStruct((PC, BAND, BINW), f32),
        in_specs=[smem] + [vmem] * 4 + [hbm, vmem],
        out_specs=hbm,
        scratch_shapes=[
            pltpu.VMEM((64, 128), bf16),
            pltpu.VMEM((FW, 128), bf16),
            pltpu.VMEM((4, PC, BAND), f32),
            pltpu.VMEM((8, 9, PC, PC), f32),
            pltpu.VMEM((8, 192, 192), bf16),
            pltpu.VMEM((8, PC, 128), f32),
            pltpu.VMEM((PC, W1), f32),
            pltpu.VMEM((PC, FW), f32),
            pltpu.VMEM((R1, PC, W1), f32),
            pltpu.VMEM((R1, 2 * PC, W1), bf16),
            pltpu.VMEM((R1, 2 * PC, W1), bf16),
            pltpu.VMEM((DIAGS, PC, W1), f32),
            pltpu.VMEM((R2, PC, W2), f32),
            pltpu.VMEM((R2, 2 * PC, W2), bf16),
            pltpu.VMEM((R2, 2 * PC, W2), bf16),
            pltpu.VMEM((BAND, PC, BINW), f32),
            pltpu.VMEM((3, HALO, 2 * PC, W1), bf16),
            pltpu.VMEM((3, HALO, 2 * PC, W2), bf16),
            dma, dma((7,)), dma((8,)), dma((3,)), dma((4,)), dma((3,)), dma((3,)), dma((6,)), dma((6,)), dma((BAND,)),
        ],
        compiler_params=pltpu.CompilerParams(
            collective_id=0, has_side_effects=True, vmem_limit_bytes=46 * 2 ** 20),
        name="trunk",
    )(dilations, features, deleted.reshape(1, 64), proj_weight.T, distance_embed, conv_weight, conv_bias.reshape(8, 1, PC))


def solution(mesh):
    return jax.shard_map(
        body,
        mesh=mesh,
        in_specs=(
            P(("rows", "band"), None),
            P(("rows", "band")),
            P(),
            P(None, "band"),
            P(),
            P(),
            P(),
        ),
        out_specs=P(None, "band", "rows"),
        check_vma=False,
    )
```

```python
import jax
import jax.numpy as jnp
from jax import lax
from jax.experimental import pallas as pl
from jax.experimental.pallas import tpu as pltpu
from jax.sharding import PartitionSpec as P

PC = 32
DIAGS = 128
HALF = 64
BAND = 32
BINW = 256
MAXDIL = 8
BINS = 8192
W1 = 512
W2 = 384
FW = 512
HALO = 8
R1 = 80
R2 = 72
ROWS = 32
MESH = pl.DeviceIdType.MESH


def split_store(y_ref, j, x):
    hi = x.astype(jnp.bfloat16)
    lo = (x - hi.astype(jnp.float32)).astype(jnp.bfloat16)
    y_ref[j, 0:PC, :] = hi
    y_ref[j, PC:2 * PC, :] = lo


def gather_taps(p, k, bias):
    width = p.shape[1]
    parts = [p[64 * b:64 * b + 32] + p[64 * b + 32:64 * b + 64] for b in range(3)]
    return (
        parts[1]
        + pltpu.roll(parts[0], k, 1)
        + pltpu.roll(parts[2], width - k, 1)
        + bias
    )


def valid_of(u, bins):
    low = jnp.maximum(0, HALF - u)
    high = jnp.where((u >= 0) & (u < DIAGS), jnp.minimum(BINS, BINS + HALF - u), 0)
    return (bins >= low) & (bins < high)


def conv_rows(ctx, base, count, sink):
    k, weights, bias, src, u0, bins = ctx
    width = bins.shape[1]
    cat = 2 if width % 256 else 1
    for g in range(0, count, cat):
        stack = [
            jnp.concatenate([src[q - k], src[q], src[q + k]], axis=0)
            for q in [base + g + c for c in range(cat)]
        ]
        stack = stack[0] if cat == 1 else jnp.concatenate(stack, axis=1)
        p = jnp.dot(weights, stack, preferred_element_type=jnp.float32)
        for c in range(cat):
            q = base + g + c
            branch = gather_taps(p[:, c * width:(c + 1) * width], k, bias)
            sink(q, jnp.where(valid_of(u0 + q, bins), branch, 0.0))


def trunk(dil_ref, feat_in, del_in, proj_in, emb_in, cw_in, cb_in, out_ref,
          feat_ref, del_ref, proj_ref, emb_ref, cw_ref, cb_ref, in_sem,
          kept, land, emb_land, w_ref, bias_ref, row_s, col_s, v_ref, ya, yb, m_ref, v2_ref, ya2, yb2, o_ref, halo1, halo2,
          send, recv, esend, erecv, msend, mrecv, hsend, hrecv, osem):
    row = lax.axis_index("rows")
    band = lax.axis_index("band")
    arguments = ((feat_in, feat_ref), (del_in, del_ref), (emb_in, emb_ref), (proj_in, proj_ref), (cb_in, cb_ref), (cw_in, cw_ref))
    fetch = [pltpu.make_async_copy(src, dst, in_sem.at[i]) for i, (src, dst) in enumerate(arguments)]
    for copy in fetch:
        copy.start()
    near = [(row, lax.rem(band + d, 4)) for d in range(1, 4)]
    upper = lax.div(band, 2)
    far_row = jnp.clip(row + 2 * upper - 1, 0, ROWS - 1)
    far = far_row != row
    barrier = pltpu.get_barrier_semaphore()

    def greet(r, b):
        pl.semaphore_signal(barrier, inc=1, device_id={"rows": r, "band": b}, device_id_type=MESH)

    for r, b in near:
        greet(r, b)

    @pl.when(row > 0)
    def _():
        greet(row - 1, 2)
        greet(row - 1, 3)

    @pl.when(row < ROWS - 1)
    def _():
        greet(row + 1, 0)
        greet(row + 1, 1)

    fetch[0].wait()
    fetch[1].wait()
    same = lax.broadcasted_iota(jnp.int32, (64, 64), 0) == lax.broadcasted_iota(jnp.int32, (64, 64), 1)
    gone = jnp.sum(jnp.where(same, del_ref[...].astype(jnp.float32), 0.0), axis=1, keepdims=True)
    kept[...] = (feat_ref[...].astype(jnp.float32) * (1.0 - gone)).astype(jnp.bfloat16)

    fetch[2].wait()
    pl.semaphore_wait(barrier, jnp.where(far, 7, 3))

    def slot(i):
        return land.at[pl.ds(64 * i, 64)]

    def send_to(r, b, to, index):
        return pltpu.make_async_remote_copy(
            kept, slot(to), send.at[index], recv.at[to],
            device_id={"rows": r, "band": b}, device_id_type=MESH)

    def send_far(d):
        return send_to(far_row, d, lax.rem(band + 6, 8), 3 + d)

    def send_emb(d, r, b):
        return pltpu.make_async_remote_copy(
            emb_ref, emb_land.at[band], esend.at[d], erecv.at[band],
            device_id={"rows": r, "band": b}, device_id_type=MESH)

    @pl.when(far)
    def _():
        for d in range(4):
            send_far(d).start()

    for d, (r, b) in enumerate(near):
        send_to(r, b, 2 + band, d).start()
    for d, (r, b) in enumerate(near):
        send_emb(d, r, b).start()
    land[pl.ds(128 + 64 * band, 64), :] = kept[...]
    emb_land[band] = emb_ref[...]
    none = jnp.zeros((128, 128), jnp.bfloat16)

    @pl.when(row == 0)
    def _():
        land[0:128] = none

    @pl.when(row == ROWS - 1)
    def _():
        land[384:512] = none

    square = lax.broadcasted_iota(jnp.int32, (PC, PC), 0) == lax.broadcasted_iota(jnp.int32, (PC, PC), 1)

    def weights(n, carry):
        for b in range(3):
            t = [cw_ref[n, 3 * a + b] for a in range(3)]
            wide = jnp.concatenate([t[0], t[0], t[1], t[1], t[2], t[2]], axis=1)
            high = wide.astype(jnp.bfloat16)
            w_ref[n, 64 * b:64 * b + 32, :] = high
            w_ref[n, 64 * b + 32:64 * b + 64, :] = (wide - high.astype(jnp.float32)).astype(jnp.bfloat16)
        column = jnp.sum(jnp.where(square, cb_ref[n], 0.0), axis=1, keepdims=True)
        bias_ref[n] = jnp.broadcast_to(column, (PC, 128))
        return carry

    for copy in fetch[3:]:
        copy.wait()
    lax.fori_loop(0, 8, weights, 0)
    zero = jnp.zeros((HALO, 2 * PC, W1), jnp.bfloat16)
    for y in (ya, yb):
        y[0:HALO] = zero
        y[R1 - HALO:] = zero

    def arrived(buf, sem):
        pltpu.make_async_copy(buf, buf, sem).wait()

    for d in range(1, 4):
        b = lax.rem(band + d, 4)
        arrived(slot(2 + b), recv.at[2 + b])
        arrived(emb_land.at[b], erecv.at[b])

    @pl.when(row > 0)
    def _():
        for i in (0, 1):
            arrived(slot(i), recv.at[i])

    @pl.when(row < ROWS - 1)
    def _():
        for i in (6, 7):
            arrived(slot(i), recv.at[i])

    half = lax.rem(band, 2)
    pair = lax.div(band, 2)
    other = band + 1 - 2 * half
    u0 = 64 * half - HALO
    skip = 128 - 128 * pair
    bin0 = row * BINW - 160 + 64 * pair
    projected = lax.dot_general(
        proj_ref[...], land[...], (((1,), (1,)), ((), ())), preferred_element_type=jnp.float32
    )
    row_s[...] = pltpu.roll(projected[:PC], 32 + (W1 - 64) * pair, 1)
    col_s[...] = projected[PC:]
    bins = lax.broadcasted_iota(jnp.int32, (1, W1), 1) + bin0
    lanes = lax.broadcasted_iota(jnp.int32, (PC, BAND), 1)

    def start_rows(t, carry):
        for s in range(24):
            q = HALO - HALO * half + t * 24 + s
            u = u0 + q
            col = pltpu.roll(col_s[...], lax.rem(2 * W1 + 96 - 64 * pair - u, W1), 1)
            emb = jnp.where(lanes == (u & 31), emb_land[u >> 5], 0.0)
            x = jnp.maximum(row_s[...] + col + jnp.sum(emb, axis=1, keepdims=True), 0.0)
            x = jnp.where(valid_of(u, bins), x, 0.0)
            v_ref[q] = x
            split_store(ya, q, x)
        return carry

    lax.fori_loop(0, 3, start_rows, 0)

    def context(n, src, u0, bins):
        bias = jnp.concatenate([bias_ref[n]] * (bins.shape[1] // 128), axis=1)
        return dil_ref[n // 2], w_ref[n], bias, src, u0, bins

    def branch_to(v, dst, residual):
        def sink(q, value):
            if residual:
                value = v[q] + value
                v[q] = value
            split_store(dst, q, jnp.maximum(value, 0.0))
        return sink

    def to_other(src, dst, ssem, rsem):
        return pltpu.make_async_remote_copy(
            src, dst, ssem, rsem, device_id={"rows": row, "band": other}, device_id_type=MESH)

    def edge1(n, dst):
        edge = dst.at[pl.ds(64 - 56 * half, HALO)]
        return to_other(edge, halo1.at[n], hsend.at[n], hrecv.at[n])

    for n in range(3):
        src, dst = (ya, yb) if n % 2 == 0 else (yb, ya)
        if n:
            edge1(n - 1, src).wait()
            src[pl.ds(72 - 72 * half, HALO)] = halo1[n - 1]
        ctx = context(n, src, u0, bins)
        sink = branch_to(v_ref, dst, n == 1)

        conv_rows(ctx, 40 - 32 * half, 32, sink)
        edge1(n, dst).start()
        conv_rows(ctx, 8 + 32 * half, 32, sink)

    edge1(2, yb).wait()
    yb[pl.ds(72 - 72 * half, HALO)] = halo1[2]
    ctx3 = context(3, yb, u0, bins)

    def swap(t, core, count):
        at = 64 * core + (16 * t if count == 16 else 32) * pair + (48 - 16 * t if count == 16 else 20) * (1 - pair)
        rows = m_ref.at[pl.ds(at, count)]
        return to_other(rows, rows, msend.at[t], mrecv.at[t])

    def keep(q, value):
        m_ref[u0 + q] = v_ref[q] + value

    def last_step(t, carry):
        conv_rows(ctx3, HALO + 16 * t * pair + (48 - 16 * t) * (1 - pair), 16, keep)

        @pl.when(t < 2)
        def _():
            swap(t, half, 16).start()

        @pl.when(t == 2)
        def _():
            swap(2, half, 12).start()

        return carry

    lax.fori_loop(0, 4, last_step, 0)
    u2 = band * BAND - 32 + 24 * half
    bins2 = lax.broadcasted_iota(jnp.int32, (1, W2), 1) + (bin0 + skip)

    def mirror_rows(start):
        for s in range(8):
            q = start + s
            u = u2 + q
            ui = jnp.clip(u, 0, DIAGS - 1)
            own = m_ref[ui, :, pl.ds(pl.multiple_of(skip, 128), W2)]
            partner = m_ref[jnp.clip(DIAGS - u, 0, DIAGS - 1)]
            partner = pltpu.roll(partner, lax.rem(W1 + HALF - skip - ui + W1, W1), 1)[:, :W2]
            partner = jnp.where(u > 0, partner, 0.0)
            x = jnp.where(valid_of(u, bins2), 0.5 * (own + partner), 0.0)
            v2_ref[q] = x
            split_store(ya2, q, jnp.maximum(x, 0.0))

    ready = (((24, 32), (32, 40), (40, 48)), ((8, 16), (16, 24), (48, 56), (56, 64)), ((0, 0), (64, 8)))
    for t in range(3):
        swap(t, 1 - half, 16 if t < 2 else 12).wait_recv()
        for low, high in ready[t]:
            mirror_rows(low + (high - low) * half)
    for t in range(3):
        swap(t, half, 16 if t < 2 else 12).wait_send()

    def edge2(n, dst):
        edge = dst.at[pl.ds(56 - 48 * half, HALO)]
        return to_other(edge, halo2.at[n], hsend.at[3 + n], hrecv.at[3 + n])

    def land2(n, y):
        edge2(n, y).wait()
        y[pl.ds(64 - 64 * half, HALO)] = halo2[n]

    def rows2(ctx, low, high, count, sink):
        conv_rows(ctx, low + (high - low) * half, count, sink)

    ctx, sink = context(4, ya2, u2, bins2), branch_to(v2_ref, yb2, False)
    rows2(ctx, 40, 8, 24, sink)
    edge2(0, yb2).start()
    rows2(ctx, 8, 32, 32, sink)
    ctx, sink = context(5, yb2, u2, bins2), branch_to(v2_ref, ya2, True)
    rows2(ctx, 16, 24, 32, sink)
    land2(0, yb2)
    rows2(ctx, 48, 8, 16, sink)
    edge2(1, ya2).start()
    ctx, sink = context(6, ya2, u2, bins2), branch_to(v2_ref, yb2, False)
    rows2(ctx, 24, 24, 24, sink)
    land2(1, ya2)
    rows2(ctx, 48, 8, 16, sink)
    edge2(2, yb2).start()

    shift = W2 - 32 - 64 * pair
    first = 32 - 24 * half
    ctx7 = context(7, yb2, u2, bins2)

    def emit(q, value):
        o_ref[q - first] = pltpu.roll(v2_ref[q] + value, shift, 1)[:, :BINW]

    def out_copy(j):
        return pltpu.make_async_copy(o_ref.at[j], out_ref.at[:, j, :], osem.at[j])

    def finish(low, high, count):
        rows2(ctx7, low, high, count, emit)
        for r in range(count):
            out_copy(low + (high - low) * half - first + r).start()

    finish(32, 16, 24)
    land2(2, yb2)
    finish(56, 8, 8)
    for j in range(BAND):
        out_copy(j).wait()
    for d, (r, b) in enumerate(near):
        send_to(r, b, 2 + band, d).wait_send()
        send_emb(d, r, b).wait_send()

    @pl.when(far)
    def _():
        for d in range(4):
            send_far(d).wait_send()


smem = pl.BlockSpec(memory_space=pltpu.SMEM)
hbm = pl.BlockSpec(memory_space=pl.ANY)
f32 = jnp.float32
bf16 = jnp.bfloat16


def body(features, deleted, proj_weight, distance_embed, conv_weight, conv_bias, dilations):
    dma = pltpu.SemaphoreType.DMA
    return pl.pallas_call(
        trunk,
        out_shape=pltpu.VMEM((PC, BAND, BINW), f32),
        in_specs=[smem] + [pl.BlockSpec(memory_space=pltpu.HBM)] * 6,
        out_specs=hbm,
        scratch_shapes=[
            pltpu.VMEM((64, 128), bf16),
            pltpu.VMEM((1, 64), jnp.int32),
            pltpu.VMEM((2 * PC, 128), bf16),
            pltpu.VMEM((PC, BAND), f32),
            pltpu.VMEM((8, 9, PC, PC), f32),
            pltpu.VMEM((8, 1, PC), f32),
            dma((6,)),
            pltpu.VMEM((64, 128), bf16),
            pltpu.VMEM((FW, 128), bf16),
            pltpu.VMEM((4, PC, BAND), f32),
            pltpu.VMEM((8, 192, 192), bf16),
            pltpu.VMEM((8, PC, 128), f32),
            pltpu.VMEM((PC, W1), f32),
            pltpu.VMEM((PC, FW), f32),
            pltpu.VMEM((R1, PC, W1), f32),
            pltpu.VMEM((R1, 2 * PC, W1), bf16),
            pltpu.VMEM((R1, 2 * PC, W1), bf16),
            pltpu.VMEM((DIAGS, PC, W1), f32),
            pltpu.VMEM((R2, PC, W2), f32),
            pltpu.VMEM((R2, 2 * PC, W2), bf16),
            pltpu.VMEM((R2, 2 * PC, W2), bf16),
            pltpu.VMEM((BAND, PC, BINW), f32),
            pltpu.VMEM((3, HALO, 2 * PC, W1), bf16),
            pltpu.VMEM((3, HALO, 2 * PC, W2), bf16),
            dma((7,)), dma((8,)), dma((3,)), dma((4,)), dma((3,)), dma((3,)), dma((6,)), dma((6,)), dma((BAND,)),
        ],
        compiler_params=pltpu.CompilerParams(
            collective_id=0, has_side_effects=True, vmem_limit_bytes=55 * 2 ** 20),
        name="trunk",
    )(dilations, features, deleted.reshape(1, 64), proj_weight.T, distance_embed, conv_weight, conv_bias.reshape(8, 1, PC))


def solution(mesh):
    return jax.shard_map(
        body,
        mesh=mesh,
        in_specs=(
            P(("rows", "band"), None),
            P(("rows", "band")),
            P(),
            P(None, "band"),
            P(),
            P(),
            P(),
        ),
        out_specs=P(None, "band", "rows"),
        check_vma=False,
    )
```

```python
import jax
import jax.numpy as jnp
from jax import lax
from jax.experimental import pallas as pl
from jax.experimental.pallas import tpu as pltpu
from jax.sharding import PartitionSpec as P

PC = 32
DIAGS = 128
HALF = 64
BAND = 32
BINW = 256
MAXDIL = 8
BINS = 8192
W1 = 512
W2 = 384
FW = 512
HALO = 8
R1 = 80
R2 = 72
ROWS = 32
MESH = pl.DeviceIdType.MESH


def split_store(y_ref, j, x):
    hi = x.astype(jnp.bfloat16)
    lo = (x - hi.astype(jnp.float32)).astype(jnp.bfloat16)
    y_ref[j, 0:PC, :] = hi
    y_ref[j, PC:2 * PC, :] = lo


def gather_taps(p, k, bias):
    width = p.shape[1]
    parts = [p[64 * b:64 * b + 32] + p[64 * b + 32:64 * b + 64] for b in range(3)]
    return (
        parts[1]
        + pltpu.roll(parts[0], k, 1)
        + pltpu.roll(parts[2], width - k, 1)
        + bias
    )


def valid_of(u, bins):
    low = jnp.maximum(0, HALF - u)
    high = jnp.where((u >= 0) & (u < DIAGS), jnp.minimum(BINS, BINS + HALF - u), 0)
    return (bins >= low) & (bins < high)


def conv_rows(ctx, base, count, sink):
    k, weights, bias, src, u0, bins = ctx
    width = bins.shape[1]
    cat = 2 if width % 256 else 1
    for g in range(0, count, cat):
        stack = [
            jnp.concatenate([src[q - k], src[q], src[q + k]], axis=0)
            for q in [base + g + c for c in range(cat)]
        ]
        stack = stack[0] if cat == 1 else jnp.concatenate(stack, axis=1)
        p = jnp.dot(weights, stack, preferred_element_type=jnp.float32)
        for c in range(cat):
            q = base + g + c
            branch = gather_taps(p[:, c * width:(c + 1) * width], k, bias)
            sink(q, jnp.where(valid_of(u0 + q, bins), branch, 0.0))


def trunk(dil_ref, feat_in, del_in, proj_in, emb_in, cw_in, cb_in, out_ref,
          feat_ref, del_ref, proj_ref, emb_ref, cw_ref, cb_ref, in_sem,
          kept, land, emb_land, emb_s, w_ref, bias_ref, row_s, col_s, v_ref, ya, yb, m_ref, v2_ref, ya2, yb2, halo1, halo2,
          send, recv, esend, erecv, msend, mrecv, hsend, hrecv):
    row = lax.axis_index("rows")
    band = lax.axis_index("band")
    near = [(row, lax.rem(band + d, 4)) for d in range(1, 4)]
    upper = lax.div(band, 2)
    far_row = jnp.clip(row + 2 * upper - 1, 0, ROWS - 1)
    far = far_row != row
    barrier = pltpu.get_barrier_semaphore()

    def greet(r, b):
        pl.semaphore_signal(barrier, inc=1, device_id={"rows": r, "band": b}, device_id_type=MESH)

    for r, b in near:
        greet(r, b)

    @pl.when(row > 0)
    def _():
        greet(row - 1, 2)
        greet(row - 1, 3)

    @pl.when(row < ROWS - 1)
    def _():
        greet(row + 1, 0)
        greet(row + 1, 1)

    arguments = ((feat_in, feat_ref), (del_in, del_ref), (emb_in, emb_ref), (proj_in, proj_ref), (cb_in, cb_ref), (cw_in, cw_ref))
    fetch = [pltpu.make_async_copy(src, dst, in_sem.at[i]) for i, (src, dst) in enumerate(arguments)]
    for copy in fetch:
        copy.start()
    fetch[0].wait()
    fetch[1].wait()
    same = lax.broadcasted_iota(jnp.int32, (64, 64), 0) == lax.broadcasted_iota(jnp.int32, (64, 64), 1)
    gone = jnp.sum(jnp.where(same, del_ref[...].astype(jnp.float32), 0.0), axis=1, keepdims=True)
    kept[...] = (feat_ref[...].astype(jnp.float32) * (1.0 - gone)).astype(jnp.bfloat16)

    fetch[2].wait()
    pl.semaphore_wait(barrier, jnp.where(far, 7, 3))

    def slot(i):
        return land.at[pl.ds(64 * i, 64)]

    def send_to(r, b, to, index):
        return pltpu.make_async_remote_copy(
            kept, slot(to), send.at[index], recv.at[to],
            device_id={"rows": r, "band": b}, device_id_type=MESH)

    def send_far(d):
        return send_to(far_row, d, lax.rem(band + 6, 8), 3 + d)

    def send_emb(d, r, b):
        return pltpu.make_async_remote_copy(
            emb_ref, emb_land.at[band], esend.at[d], erecv.at[band],
            device_id={"rows": r, "band": b}, device_id_type=MESH)

    @pl.when(far)
    def _():
        for d in range(4):
            send_far(d).start()

    for d, (r, b) in enumerate(near):
        send_to(r, b, 2 + band, d).start()
    for d, (r, b) in enumerate(near):
        send_emb(d, r, b).start()
    land[pl.ds(128 + 64 * band, 64), :] = kept[...]
    emb_land[band] = emb_ref[...]
    none = jnp.zeros((128, 128), jnp.bfloat16)

    @pl.when(row == 0)
    def _():
        land[0:128] = none

    @pl.when(row == ROWS - 1)
    def _():
        land[384:512] = none

    square = lax.broadcasted_iota(jnp.int32, (PC, PC), 0) == lax.broadcasted_iota(jnp.int32, (PC, PC), 1)

    def weights(n, carry):
        for b in range(3):
            t = [cw_ref[n, 3 * a + b] for a in range(3)]
            wide = jnp.concatenate([t[0], t[0], t[1], t[1], t[2], t[2]], axis=1)
            high = wide.astype(jnp.bfloat16)
            w_ref[n, 64 * b:64 * b + 32, :] = high
            w_ref[n, 64 * b + 32:64 * b + 64, :] = (wide - high.astype(jnp.float32)).astype(jnp.bfloat16)
        column = jnp.sum(jnp.where(square, cb_ref[n], 0.0), axis=1, keepdims=True)
        bias_ref[n] = jnp.broadcast_to(column, (PC, 128))
        return carry

    for copy in fetch[3:]:
        copy.wait()
    lax.fori_loop(0, 8, weights, 0)
    zero = jnp.zeros((HALO, 2 * PC, W1), jnp.bfloat16)
    for y in (ya, yb):
        y[0:HALO] = zero
        y[R1 - HALO:] = zero

    def arrived(buf, sem):
        pltpu.make_async_copy(buf, buf, sem).wait()

    half = lax.rem(band, 2)
    pair = lax.div(band, 2)
    other = band + 1 - 2 * half
    u0 = 64 * half - HALO
    first_q = HALO - HALO * half
    for d in range(1, 4):
        b = lax.rem(band + d, 4)
        arrived(emb_land.at[b], erecv.at[b])

    lanes = lax.broadcasted_iota(jnp.int32, (PC, BAND), 1)

    def spread(t, carry):
        for s in range(24):
            q = first_q + t * 24 + s
            u = u0 + q
            emb = jnp.where(lanes == (u & 31), emb_land[u >> 5], 0.0)
            emb_s[q] = jnp.broadcast_to(jnp.sum(emb, axis=1, keepdims=True), (PC, 128))
        return carry

    lax.fori_loop(0, 3, spread, 0)
    for d in range(1, 4):
        b = lax.rem(band + d, 4)
        arrived(slot(2 + b), recv.at[2 + b])

    @pl.when(row > 0)
    def _():
        for i in (0, 1):
            arrived(slot(i), recv.at[i])

    @pl.when(row < ROWS - 1)
    def _():
        for i in (6, 7):
            arrived(slot(i), recv.at[i])

    skip = 128 - 128 * pair
    bin0 = row * BINW - 160 + 64 * pair
    projected = lax.dot_general(
        proj_ref[...], land[...], (((1,), (1,)), ((), ())), preferred_element_type=jnp.float32
    )
    row_s[...] = pltpu.roll(projected[:PC], 32 + (W1 - 64) * pair, 1)
    col_s[...] = projected[PC:]
    bins = lax.broadcasted_iota(jnp.int32, (1, W1), 1) + bin0

    def start_rows(t, carry):
        for s in range(24):
            q = first_q + t * 24 + s
            u = u0 + q
            col = pltpu.roll(col_s[...], lax.rem(2 * W1 + 96 - 64 * pair - u, W1), 1)
            emb = jnp.concatenate([emb_s[q]] * (W1 // 128), axis=1)
            x = jnp.maximum(row_s[...] + col + emb, 0.0)
            x = jnp.where(valid_of(u, bins), x, 0.0)
            v_ref[q] = x
            split_store(ya, q, x)
        return carry

    lax.fori_loop(0, 3, start_rows, 0)

    def context(n, src, u0, bins):
        bias = jnp.concatenate([bias_ref[n]] * (bins.shape[1] // 128), axis=1)
        return dil_ref[n // 2], w_ref[n], bias, src, u0, bins

    def branch_to(v, dst, residual):
        def sink(q, value):
            if residual:
                value = v[q] + value
                v[q] = value
            split_store(dst, q, jnp.maximum(value, 0.0))
        return sink

    def to_other(src, dst, ssem, rsem):
        return pltpu.make_async_remote_copy(
            src, dst, ssem, rsem, device_id={"rows": row, "band": other}, device_id_type=MESH)

    def edge1(n, dst):
        edge = dst.at[pl.ds(64 - 56 * half, HALO)]
        return to_other(edge, halo1.at[n], hsend.at[n], hrecv.at[n])

    for n in range(3):
        src, dst = (ya, yb) if n % 2 == 0 else (yb, ya)
        if n:
            edge1(n - 1, src).wait()
            src[pl.ds(72 - 72 * half, HALO)] = halo1[n - 1]
        ctx = context(n, src, u0, bins)
        sink = branch_to(v_ref, dst, n == 1)

        conv_rows(ctx, 40 - 32 * half, 32, sink)
        edge1(n, dst).start()
        conv_rows(ctx, 8 + 32 * half, 32, sink)

    edge1(2, yb).wait()
    yb[pl.ds(72 - 72 * half, HALO)] = halo1[2]
    ctx3 = context(3, yb, u0, bins)

    def swap(t, core, count):
        at = 64 * core + (16 * t if count == 16 else 32) * pair + (48 - 16 * t if count == 16 else 20) * (1 - pair)
        rows = m_ref.at[pl.ds(at, count)]
        return to_other(rows, rows, msend.at[t], mrecv.at[t])

    def keep(q, value):
        m_ref[u0 + q] = v_ref[q] + value

    for t in range(4):
        conv_rows(ctx3, HALO + 16 * t * pair + (48 - 16 * t) * (1 - pair), 16, keep)
        if t < 3:
            swap(t, half, 16 if t < 2 else 12).start()

    u2 = band * BAND - 32 + 24 * half
    bins2 = lax.broadcasted_iota(jnp.int32, (1, W2), 1) + (bin0 + skip)

    def mirror_rows(start):
        for s in range(8):
            q = start + s
            u = u2 + q
            ui = jnp.clip(u, 0, DIAGS - 1)
            own = m_ref[ui, :, pl.ds(pl.multiple_of(skip, 128), W2)]
            partner = m_ref[jnp.clip(DIAGS - u, 0, DIAGS - 1)]
            partner = pltpu.roll(partner, lax.rem(W1 + HALF - skip - ui + W1, W1), 1)[:, :W2]
            partner = jnp.where(u > 0, partner, 0.0)
            x = jnp.where(valid_of(u, bins2), 0.5 * (own + partner), 0.0)
            v2_ref[q] = x
            split_store(ya2, q, jnp.maximum(x, 0.0))

    ready = (((24, 32), (32, 40), (40, 48)), ((8, 16), (16, 24), (48, 56), (56, 64)), ((0, 0), (64, 8)))
    for t in range(3):
        swap(t, 1 - half, 16 if t < 2 else 12).wait_recv()
        for low, high in ready[t]:
            mirror_rows(low + (high - low) * half)
    for t in range(3):
        swap(t, half, 16 if t < 2 else 12).wait_send()

    def edge2(n, dst):
        edge = dst.at[pl.ds(56 - 48 * half, HALO)]
        return to_other(edge, halo2.at[n], hsend.at[3 + n], hrecv.at[3 + n])

    def land2(n, y):
        edge2(n, y).wait()
        y[pl.ds(64 - 64 * half, HALO)] = halo2[n]

    def rows2(ctx, low, high, count, sink):
        conv_rows(ctx, low + (high - low) * half, count, sink)

    ctx, sink = context(4, ya2, u2, bins2), branch_to(v2_ref, yb2, False)
    rows2(ctx, 40, 8, 24, sink)
    edge2(0, yb2).start()
    rows2(ctx, 8, 32, 32, sink)
    ctx, sink = context(5, yb2, u2, bins2), branch_to(v2_ref, ya2, True)
    rows2(ctx, 16, 24, 32, sink)
    land2(0, yb2)
    rows2(ctx, 48, 8, 16, sink)
    edge2(1, ya2).start()
    ctx, sink = context(6, ya2, u2, bins2), branch_to(v2_ref, yb2, False)
    rows2(ctx, 24, 24, 24, sink)
    land2(1, ya2)
    rows2(ctx, 48, 8, 16, sink)
    edge2(2, yb2).start()

    shift = W2 - 32 - 64 * pair
    first = 32 - 24 * half
    ctx7 = context(7, yb2, u2, bins2)

    def emit(q, value):
        out_ref[:, q - first, :] = pltpu.roll(v2_ref[q] + value, shift, 1)[:, :BINW]

    rows2(ctx7, 32, 16, 24, emit)
    land2(2, yb2)
    rows2(ctx7, 56, 8, 8, emit)
    for d, (r, b) in enumerate(near):
        send_to(r, b, 2 + band, d).wait_send()
        send_emb(d, r, b).wait_send()

    @pl.when(far)
    def _():
        for d in range(4):
            send_far(d).wait_send()


smem = pl.BlockSpec(memory_space=pltpu.SMEM)
f32 = jnp.float32
bf16 = jnp.bfloat16


def body(features, deleted, proj_weight, distance_embed, conv_weight, conv_bias, dilations):
    dma = pltpu.SemaphoreType.DMA
    return pl.pallas_call(
        trunk,
        out_shape=pltpu.VMEM((PC, BAND, BINW), f32),
        in_specs=[smem] + [pl.BlockSpec(memory_space=pltpu.HBM)] * 6,
        out_specs=pl.BlockSpec(memory_space=pltpu.VMEM),
        scratch_shapes=[
            pltpu.VMEM((64, 128), bf16),
            pltpu.VMEM((1, 64), jnp.int32),
            pltpu.VMEM((2 * PC, 128), bf16),
            pltpu.VMEM((PC, BAND), f32),
            pltpu.VMEM((8, 9, PC, PC), f32),
            pltpu.VMEM((8, 1, PC), f32),
            dma((6,)),
            pltpu.VMEM((64, 128), bf16),
            pltpu.VMEM((FW, 128), bf16),
            pltpu.VMEM((4, PC, BAND), f32),
            pltpu.VMEM((R1, PC, 128), f32),
            pltpu.VMEM((8, 192, 192), bf16),
            pltpu.VMEM((8, PC, 128), f32),
            pltpu.VMEM((PC, W1), f32),
            pltpu.VMEM((PC, FW), f32),
            pltpu.VMEM((R1, PC, W1), f32),
            pltpu.VMEM((R1, 2 * PC, W1), bf16),
            pltpu.VMEM((R1, 2 * PC, W1), bf16),
            pltpu.VMEM((DIAGS, PC, W1), f32),
            pltpu.VMEM((R2, PC, W2), f32),
            pltpu.VMEM((R2, 2 * PC, W2), bf16),
            pltpu.VMEM((R2, 2 * PC, W2), bf16),
            pltpu.VMEM((3, HALO, 2 * PC, W1), bf16),
            pltpu.VMEM((3, HALO, 2 * PC, W2), bf16),
            dma((7,)), dma((8,)), dma((3,)), dma((4,)), dma((3,)), dma((3,)), dma((6,)), dma((6,)),
        ],
        compiler_params=pltpu.CompilerParams(
            collective_id=0, has_side_effects=True, vmem_limit_bytes=55 * 2 ** 20),
        name="trunk",
    )(dilations, features, deleted.reshape(1, 64), proj_weight.T, distance_embed, conv_weight, conv_bias.reshape(8, 1, PC))


def solution(mesh):
    return jax.shard_map(
        body,
        mesh=mesh,
        in_specs=(
            P(("rows", "band"), None),
            P(("rows", "band")),
            P(),
            P(None, "band"),
            P(),
            P(),
            P(),
        ),
        out_specs=P(None, "band", "rows"),
        check_vma=False,
    )
```

```python
import jax
import jax.numpy as jnp
from jax import lax
from jax.experimental import pallas as pl
from jax.experimental.pallas import tpu as pltpu
from jax.sharding import PartitionSpec as P

PC = 32
DIAGS = 128
HALF = 64
BAND = 32
BINW = 256
MAXDIL = 8
BINS = 8192
W1 = 512
W2 = 384
FW = 512
HALO = 8
R1 = 80
R2 = 72
ROWS = 32
MESH = pl.DeviceIdType.MESH


def split_store(y_ref, j, x):
    hi = x.astype(jnp.bfloat16)
    lo = (x - hi.astype(jnp.float32)).astype(jnp.bfloat16)
    y_ref[j, 0:PC, :] = hi
    y_ref[j, PC:2 * PC, :] = lo


def gather_taps(p, k, bias):
    width = p.shape[1]
    parts = [p[64 * b:64 * b + 32] + p[64 * b + 32:64 * b + 64] for b in range(3)]
    return (
        parts[1]
        + pltpu.roll(parts[0], k, 1)
        + pltpu.roll(parts[2], width - k, 1)
        + bias
    )


def valid_of(u, bins):
    low = jnp.maximum(0, HALF - u)
    high = jnp.where((u >= 0) & (u < DIAGS), jnp.minimum(BINS, BINS + HALF - u), 0)
    return (bins >= low) & (bins < high)


def conv_rows(ctx, base, count, sink):
    k, weights, bias, src, u0, bins = ctx
    width = bins.shape[1]
    cat = 2 if width % 256 else 1
    for g in range(0, count, cat):
        stack = [
            jnp.concatenate([src[q - k], src[q], src[q + k]], axis=0)
            for q in [base + g + c for c in range(cat)]
        ]
        stack = stack[0] if cat == 1 else jnp.concatenate(stack, axis=1)
        p = jnp.dot(weights, stack, preferred_element_type=jnp.float32)
        for c in range(cat):
            q = base + g + c
            branch = gather_taps(p[:, c * width:(c + 1) * width], k, bias)
            sink(q, jnp.where(valid_of(u0 + q, bins), branch, 0.0))


def trunk(dil_ref, feat_in, del_in, proj_in, emb_in, cw_in, cb_in, out_ref,
          feat_ref, del_ref, proj_ref, emb_ref, cw_ref, cb_ref, in_sem,
          kept, land, emb_land, emb_s, w_ref, bias_ref, row_s, col_s, v_ref, ya, yb, m_ref, v2_ref, ya2, yb2, halo1, halo2,
          send, recv, esend, erecv, msend, mrecv, hsend, hrecv):
    row = lax.axis_index("rows")
    band = lax.axis_index("band")
    near = [(row, lax.rem(band + d, 4)) for d in range(1, 4)]
    upper = lax.div(band, 2)
    far_row = jnp.clip(row + 2 * upper - 1, 0, ROWS - 1)
    far = far_row != row
    barrier = pltpu.get_barrier_semaphore()

    def greet(r, b):
        pl.semaphore_signal(barrier, inc=1, device_id={"rows": r, "band": b}, device_id_type=MESH)

    for r, b in near:
        greet(r, b)

    @pl.when(row > 0)
    def _():
        greet(row - 1, 2)
        greet(row - 1, 3)

    @pl.when(row < ROWS - 1)
    def _():
        greet(row + 1, 0)
        greet(row + 1, 1)

    arguments = ((feat_in, feat_ref), (del_in, del_ref), (emb_in, emb_ref), (proj_in, proj_ref), (cb_in, cb_ref), (cw_in, cw_ref))
    fetch = [pltpu.make_async_copy(src, dst, in_sem.at[i]) for i, (src, dst) in enumerate(arguments)]
    for copy in fetch:
        copy.start()
    fetch[0].wait()
    fetch[1].wait()
    same = lax.broadcasted_iota(jnp.int32, (64, 64), 0) == lax.broadcasted_iota(jnp.int32, (64, 64), 1)
    gone = jnp.sum(jnp.where(same, del_ref[...].astype(jnp.float32), 0.0), axis=1, keepdims=True)
    kept[...] = (feat_ref[...].astype(jnp.float32) * (1.0 - gone)).astype(jnp.bfloat16)

    fetch[2].wait()
    pl.semaphore_wait(barrier, jnp.where(far, 7, 3))

    def slot(i):
        return land.at[pl.ds(64 * i, 64)]

    def send_to(r, b, to, index):
        return pltpu.make_async_remote_copy(
            kept, slot(to), send.at[index], recv.at[to],
            device_id={"rows": r, "band": b}, device_id_type=MESH)

    def send_far(d):
        return send_to(far_row, d, lax.rem(band + 6, 8), 3 + d)

    def send_emb(d, r, b):
        return pltpu.make_async_remote_copy(
            emb_ref, emb_land.at[band], esend.at[d], erecv.at[band],
            device_id={"rows": r, "band": b}, device_id_type=MESH)

    for d, (r, b) in enumerate(near):
        send_emb(d, r, b).start()

    @pl.when(far)
    def _():
        for d in range(4):
            send_far(d).start()

    for d, (r, b) in enumerate(near):
        send_to(r, b, 2 + band, d).start()
    land[pl.ds(128 + 64 * band, 64), :] = kept[...]
    emb_land[band] = emb_ref[...]
    none = jnp.zeros((128, 128), jnp.bfloat16)

    @pl.when(row == 0)
    def _():
        land[0:128] = none

    @pl.when(row == ROWS - 1)
    def _():
        land[384:512] = none

    square = lax.broadcasted_iota(jnp.int32, (PC, PC), 0) == lax.broadcasted_iota(jnp.int32, (PC, PC), 1)

    def weights(n, carry):
        for b in range(3):
            t = [cw_ref[n, 3 * a + b] for a in range(3)]
            wide = jnp.concatenate([t[0], t[0], t[1], t[1], t[2], t[2]], axis=1)
            high = wide.astype(jnp.bfloat16)
            w_ref[n, 64 * b:64 * b + 32, :] = high
            w_ref[n, 64 * b + 32:64 * b + 64, :] = (wide - high.astype(jnp.float32)).astype(jnp.bfloat16)
        column = jnp.sum(jnp.where(square, cb_ref[n], 0.0), axis=1, keepdims=True)
        bias_ref[n] = jnp.broadcast_to(column, (PC, 128))
        return carry

    for copy in fetch[3:]:
        copy.wait()
    lax.fori_loop(0, 8, weights, 0)
    zero = jnp.zeros((HALO, 2 * PC, W1), jnp.bfloat16)
    for y in (ya, yb):
        y[0:HALO] = zero
        y[R1 - HALO:] = zero

    def arrived(buf, sem):
        pltpu.make_async_copy(buf, buf, sem).wait()

    half = lax.rem(band, 2)
    pair = lax.div(band, 2)
    other = band + 1 - 2 * half
    u0 = 64 * half - HALO
    first_q = HALO - HALO * half
    for d in range(1, 4):
        b = lax.rem(band + d, 4)
        arrived(emb_land.at[b], erecv.at[b])

    lanes = lax.broadcasted_iota(jnp.int32, (PC, BAND), 1)

    def spread(t, carry):
        for s in range(36):
            q = first_q + t * 36 + s
            u = u0 + q
            emb = jnp.where(lanes == (u & 31), emb_land[u >> 5], 0.0)
            emb_s[q] = jnp.broadcast_to(jnp.sum(emb, axis=1, keepdims=True), (PC, 128))
        return carry

    lax.fori_loop(0, 2, spread, 0)
    for d in range(1, 4):
        b = lax.rem(band + d, 4)
        arrived(slot(2 + b), recv.at[2 + b])

    @pl.when(row > 0)
    def _():
        for i in (0, 1):
            arrived(slot(i), recv.at[i])

    @pl.when(row < ROWS - 1)
    def _():
        for i in (6, 7):
            arrived(slot(i), recv.at[i])

    skip = 128 - 128 * pair
    bin0 = row * BINW - 160 + 64 * pair
    projected = lax.dot_general(
        proj_ref[...], land[...], (((1,), (1,)), ((), ())), preferred_element_type=jnp.float32
    )
    row_s[...] = pltpu.roll(projected[:PC], 32 + (W1 - 64) * pair, 1)
    col_s[...] = projected[PC:]
    bins = lax.broadcasted_iota(jnp.int32, (1, W1), 1) + bin0

    def start_rows(t, carry):
        for s in range(36):
            q = first_q + t * 36 + s
            u = u0 + q
            col = pltpu.roll(col_s[...], lax.rem(2 * W1 + 96 - 64 * pair - u, W1), 1)
            emb = jnp.concatenate([emb_s[q]] * (W1 // 128), axis=1)
            x = jnp.maximum(row_s[...] + col + emb, 0.0)
            x = jnp.where(valid_of(u, bins), x, 0.0)
            v_ref[q] = x
            split_store(ya, q, x)
        return carry

    lax.fori_loop(0, 2, start_rows, 0)

    def context(n, src, u0, bins):
        bias = jnp.concatenate([bias_ref[n]] * (bins.shape[1] // 128), axis=1)
        return dil_ref[n // 2], w_ref[n], bias, src, u0, bins

    def branch_to(v, dst, residual):
        def sink(q, value):
            if residual:
                value = v[q] + value
                v[q] = value
            split_store(dst, q, jnp.maximum(value, 0.0))
        return sink

    def to_other(src, dst, ssem, rsem):
        return pltpu.make_async_remote_copy(
            src, dst, ssem, rsem, device_id={"rows": row, "band": other}, device_id_type=MESH)

    def edge1(n, dst):
        edge = dst.at[pl.ds(64 - 56 * half, HALO)]
        return to_other(edge, halo1.at[n], hsend.at[n], hrecv.at[n])

    for n in range(3):
        src, dst = (ya, yb) if n % 2 == 0 else (yb, ya)
        if n:
            edge1(n - 1, src).wait()
            src[pl.ds(72 - 72 * half, HALO)] = halo1[n - 1]
        ctx = context(n, src, u0, bins)
        sink = branch_to(v_ref, dst, n == 1)

        conv_rows(ctx, 40 - 32 * half, 32, sink)
        edge1(n, dst).start()
        conv_rows(ctx, 8 + 32 * half, 32, sink)

    edge1(2, yb).wait()
    yb[pl.ds(72 - 72 * half, HALO)] = halo1[2]
    ctx3 = context(3, yb, u0, bins)

    def swap(t, core, count):
        at = 64 * core + (16 * t if count == 16 else 32) * pair + (48 - 16 * t if count == 16 else 20) * (1 - pair)
        rows = m_ref.at[pl.ds(at, count)]
        return to_other(rows, rows, msend.at[t], mrecv.at[t])

    def keep(q, value):
        m_ref[u0 + q] = v_ref[q] + value

    for t in range(4):
        conv_rows(ctx3, HALO + 16 * t * pair + (48 - 16 * t) * (1 - pair), 16, keep)
        if t < 3:
            swap(t, half, 16 if t < 2 else 12).start()

    u2 = band * BAND - 32 + 24 * half
    bins2 = lax.broadcasted_iota(jnp.int32, (1, W2), 1) + (bin0 + skip)

    def mirror_rows(start):
        for s in range(8):
            q = start + s
            u = u2 + q
            ui = jnp.clip(u, 0, DIAGS - 1)
            own = m_ref[ui, :, pl.ds(pl.multiple_of(skip, 128), W2)]
            partner = m_ref[jnp.clip(DIAGS - u, 0, DIAGS - 1)]
            partner = pltpu.roll(partner, lax.rem(W1 + HALF - skip - ui + W1, W1), 1)[:, :W2]
            partner = jnp.where(u > 0, partner, 0.0)
            x = jnp.where(valid_of(u, bins2), 0.5 * (own + partner), 0.0)
            v2_ref[q] = x
            split_store(ya2, q, jnp.maximum(x, 0.0))

    ready = (((24, 32), (32, 40), (40, 48)), ((8, 16), (16, 24), (48, 56), (56, 64)), ((0, 0), (64, 8)))
    for t in range(3):
        swap(t, 1 - half, 16 if t < 2 else 12).wait_recv()
        for low, high in ready[t]:
            mirror_rows(low + (high - low) * half)
    for t in range(3):
        swap(t, half, 16 if t < 2 else 12).wait_send()

    def edge2(n, dst):
        edge = dst.at[pl.ds(56 - 48 * half, HALO)]
        return to_other(edge, halo2.at[n], hsend.at[3 + n], hrecv.at[3 + n])

    def land2(n, y):
        edge2(n, y).wait()
        y[pl.ds(64 - 64 * half, HALO)] = halo2[n]

    def rows2(ctx, low, high, count, sink):
        conv_rows(ctx, low + (high - low) * half, count, sink)

    ctx, sink = context(4, ya2, u2, bins2), branch_to(v2_ref, yb2, False)
    rows2(ctx, 40, 8, 24, sink)
    edge2(0, yb2).start()
    rows2(ctx, 8, 32, 32, sink)
    ctx, sink = context(5, yb2, u2, bins2), branch_to(v2_ref, ya2, True)
    rows2(ctx, 16, 24, 32, sink)
    land2(0, yb2)
    rows2(ctx, 48, 8, 16, sink)
    edge2(1, ya2).start()
    ctx, sink = context(6, ya2, u2, bins2), branch_to(v2_ref, yb2, False)
    rows2(ctx, 24, 24, 24, sink)
    land2(1, ya2)
    rows2(ctx, 48, 8, 16, sink)
    edge2(2, yb2).start()

    shift = W2 - 32 - 64 * pair
    first = 32 - 24 * half
    ctx7 = context(7, yb2, u2, bins2)

    def emit(q, value):
        out_ref[:, q - first, :] = pltpu.roll(v2_ref[q] + value, shift, 1)[:, :BINW]

    rows2(ctx7, 32, 16, 24, emit)
    land2(2, yb2)
    rows2(ctx7, 56, 8, 8, emit)
    for d, (r, b) in enumerate(near):
        send_to(r, b, 2 + band, d).wait_send()
        send_emb(d, r, b).wait_send()

    @pl.when(far)
    def _():
        for d in range(4):
            send_far(d).wait_send()


smem = pl.BlockSpec(memory_space=pltpu.SMEM)
f32 = jnp.float32
bf16 = jnp.bfloat16


def body(features, deleted, proj_weight, distance_embed, conv_weight, conv_bias, dilations):
    dma = pltpu.SemaphoreType.DMA
    return pl.pallas_call(
        trunk,
        out_shape=pltpu.VMEM((PC, BAND, BINW), f32),
        in_specs=[smem] + [pl.BlockSpec(memory_space=pltpu.HBM)] * 6,
        out_specs=pl.BlockSpec(memory_space=pltpu.VMEM),
        scratch_shapes=[
            pltpu.VMEM((64, 128), bf16),
            pltpu.VMEM((1, 64), jnp.int32),
            pltpu.VMEM((2 * PC, 128), bf16),
            pltpu.VMEM((PC, BAND), f32),
            pltpu.VMEM((8, 9, PC, PC), f32),
            pltpu.VMEM((8, 1, PC), f32),
            dma((6,)),
            pltpu.VMEM((64, 128), bf16),
            pltpu.VMEM((FW, 128), bf16),
            pltpu.VMEM((4, PC, BAND), f32),
            pltpu.VMEM((R1, PC, 128), f32),
            pltpu.VMEM((8, 192, 192), bf16),
            pltpu.VMEM((8, PC, 128), f32),
            pltpu.VMEM((PC, W1), f32),
            pltpu.VMEM((PC, FW), f32),
            pltpu.VMEM((R1, PC, W1), f32),
            pltpu.VMEM((R1, 2 * PC, W1), bf16),
            pltpu.VMEM((R1, 2 * PC, W1), bf16),
            pltpu.VMEM((DIAGS, PC, W1), f32),
            pltpu.VMEM((R2, PC, W2), f32),
            pltpu.VMEM((R2, 2 * PC, W2), bf16),
            pltpu.VMEM((R2, 2 * PC, W2), bf16),
            pltpu.VMEM((3, HALO, 2 * PC, W1), bf16),
            pltpu.VMEM((3, HALO, 2 * PC, W2), bf16),
            dma((7,)), dma((8,)), dma((3,)), dma((4,)), dma((3,)), dma((3,)), dma((6,)), dma((6,)),
        ],
        compiler_params=pltpu.CompilerParams(
            collective_id=0, has_side_effects=True, vmem_limit_bytes=55 * 2 ** 20),
        name="trunk",
    )(dilations, features, deleted.reshape(1, 64), proj_weight.T, distance_embed, conv_weight, conv_bias.reshape(8, 1, PC))


def solution(mesh):
    return jax.shard_map(
        body,
        mesh=mesh,
        in_specs=(
            P(("rows", "band"), None),
            P(("rows", "band")),
            P(),
            P(None, "band"),
            P(),
            P(),
            P(),
        ),
        out_specs=P(None, "band", "rows"),
        check_vma=False,
    )
```
